32 devices in a mesh: section: 2 (over y), dp: 16 (over z, x, core).
Axes of the slice: x: 2, y: 2, z: 4, core: 2. Of those that a mesh axis runs over, the one named last changes fastest.
Arguments:
- tokens: bfloat16 [2, 16, 512, 384], P(None, 'dp'), may hold values from -6 to 6
- cotangent: bfloat16 [2, 16, 512, 384], P(None, 'dp'), may hold values from -6 to 6
- views: int32 [2, 16], P(None, 'dp'), may hold values from 2 to 8, as said below
- attn_gain: bfloat16 [2, 384], P('section'), may hold values from 0.099609375 to 1.8984375
- attn_shift: bfloat16 [2, 384], P('section'), may hold values from -1.75 to 1.75
- qkv_weight: bfloat16 [2, 384, 1152], P('section'), may hold values from -0.3125 to 0.3125
- query_bias: bfloat16 [2, 384], P('section'), may hold values from -3 to 3
- value_bias: bfloat16 [2, 384], P('section'), may hold values from -3 to 3
- out_weight: bfloat16 [2, 384, 384], P('section'), may hold values from -1.25 to 1.25
- out_bias: bfloat16 [2, 384], P('section'), may hold values from -1.75 to 1.75
- mlp_gain: bfloat16 [2, 384], P('section'), may hold values from 0.099609375 to 1.8984375
- mlp_shift: bfloat16 [2, 384], P('section'), may hold values from -1.75 to 1.75
- up_weight: bfloat16 [2, 384, 1536], P('section'), may hold values from -0.3125 to 0.3125
- up_bias: bfloat16 [2, 1536], P('section'), may hold values from -3 to 3
- down_weight: bfloat16 [2, 1536, 384], P('section'), may hold values from -0.15625 to 0.15625
- down_bias: bfloat16 [2, 384], P('section'), may hold values from -1.75 to 1.75
Outputs:
- layer_out: bfloat16 [2, 2, 16, 512, 384], P('section', None, 'dp')
- input_grads: bfloat16 [2, 2, 16, 512, 384], P('section', None, 'dp')
- grad_attn_gain: float32 [2, 384], P('section')
- grad_attn_shift: float32 [2, 384], P('section')
- grad_qkv_weight: float32 [2, 384, 1152], P('section')
- grad_query_bias: float32 [2, 384], P('section')
- grad_value_bias: float32 [2, 384], P('section')
- grad_out_weight: float32 [2, 384, 384], P('section')
- grad_out_bias: float32 [2, 384], P('section')
- grad_mlp_gain: float32 [2, 384], P('section')
- grad_mlp_shift: float32 [2, 384], P('section')
- grad_up_weight: float32 [2, 384, 1536], P('section')
- grad_up_bias: float32 [2, 1536], P('section')
- grad_down_weight: float32 [2, 1536, 384], P('section')
- grad_down_bias: float32 [2, 384], P('section')
The draws below stay inside these ranges and needn't reach their ends.
Inputs may be any that keep to these rules, and one draw needn't show every extreme that they name: In every micro-batch some scene has 8 views.
All inputs are finite; a program needn't handle non-finite values.
Results may differ from the reference program's by a relative error of at most 0.014.
Values may be sent and summed in bfloat16 or wider, within the bound.
No kernel may reach another device: no remote copies, remote signals or barrier semaphores. Data moves between devices by JAX's collectives and lax.ppermute only.
A program may use at most 192 MiB of HBM per device.

```python
import jax
import jax.numpy as jnp
from jax import lax

D = 384
HEADS = 6
HEAD = 64
FF = 1536
VIEWS = 8
PATCHES = 64
MICRO = 2
SLOTS = 512
SCENES = 16


def draw_views(key, part):
    key = jax.random.fold_in(key, 11)
    base = jax.random.randint(key, (MICRO, SCENES), 2, VIEWS + 1)
    full_pick = jax.random.randint(jax.random.fold_in(key, 1), (MICRO,), 0, SCENES)
    least_pick = jax.random.randint(jax.random.fold_in(key, 2), (MICRO,), 0, SCENES)
    places = jnp.arange(SCENES)[None, :]
    full_mask = places == full_pick[:, None]
    least_mask = places == least_pick[:, None]
    return jnp.where(full_mask, VIEWS, jnp.where(least_mask, 2, base)).astype(jnp.int32)


def levels(own_key, extent, cuts, least, top_value):
    level = 1.0
    for dim, parts in cuts:
        steps = jax.random.uniform(jax.random.fold_in(jax.random.fold_in(own_key, 6), dim), (parts,), jnp.float32, least / len(cuts), top_value / len(cuts))
        level = level * jnp.repeat(jnp.exp(steps), extent[dim] // parts).reshape((-1,) + (1,) * (len(extent) - 1 - dim))
    return level


def bell_draw(stream_key, dims, deviation, most, cuts=(), dtype=jnp.bfloat16):
    level = levels(stream_key, dims, cuts, -0.22, 0.18) if cuts else 1.0
    values = jax.random.normal(stream_key, dims, jnp.float32) * deviation * level
    return jnp.minimum(jnp.maximum(values, -most), most).astype(dtype)


def setup_inputs(seed: int = 0) -> dict:
    streams_of = jax.random.split(jax.random.key(seed), 17)
    tokens = bell_draw(streams_of[0], (MICRO, SCENES, SLOTS, D), 1.0, 6.0, ((1, 16),))
    cotangent = bell_draw(streams_of[1], (MICRO, SCENES, SLOTS, D), 1.0, 6.0, ((1, 16),))
    views = draw_views(jax.random.fold_in(streams_of[16], 71), 0)
    attn_gain = jnp.clip(1.0 + 0.18 * jax.random.normal(streams_of[3], (2, D), jnp.float32), 0.099609375, 1.8984375).astype(jnp.bfloat16)
    attn_shift = bell_draw(streams_of[4], (2, D), 0.3, 1.75, ((0, 2),))
    qkv_weight = bell_draw(streams_of[5], (2, D, 3 * D), D ** -0.5, 0.3125, ((0, 2),))
    query_bias = bell_draw(streams_of[6], (2, D), 0.5, 3.0, ((0, 2),))
    value_bias = bell_draw(streams_of[7], (2, D), 0.5, 3.0, ((0, 2),))
    out_weight = bell_draw(streams_of[8], (2, D, D), (D // 16) ** -0.5, 1.25, ((0, 2),))
    out_bias = bell_draw(streams_of[9], (2, D), 0.3, 1.75, ((0, 2),))
    mlp_gain = jnp.clip(1.0 + 0.18 * jax.random.normal(streams_of[10], (2, D), jnp.float32), 0.099609375, 1.8984375).astype(jnp.bfloat16)
    mlp_shift = bell_draw(streams_of[11], (2, D), 0.3, 1.75, ((0, 2),))
    up_weight = bell_draw(streams_of[12], (2, D, FF), D ** -0.5, 0.3125, ((0, 2),))
    up_bias = bell_draw(streams_of[13], (2, FF), 0.5, 3.0, ((0, 2),))
    down_weight = bell_draw(streams_of[14], (2, FF, D), FF ** -0.5, 0.15625, ((0, 2),))
    down_bias = bell_draw(streams_of[15], (2, D), 0.3, 1.75, ((0, 2),))
    return {"tokens": tokens, "cotangent": cotangent, "views": views, "attn_gain": attn_gain, "attn_shift": attn_shift, "qkv_weight": qkv_weight, "query_bias": query_bias, "value_bias": value_bias, "out_weight": out_weight, "out_bias": out_bias, "mlp_gain": mlp_gain, "mlp_shift": mlp_shift, "up_weight": up_weight, "up_bias": up_bias, "down_weight": down_weight, "down_bias": down_bias}


@jax.custom_vjp
def low(v):
    return lax.optimization_barrier(v.astype(jnp.bfloat16)).astype(jnp.float32)

@jax.custom_vjp
def low_back(v):
    return v

def low_keep(v):
    return (low(v), None)

def low_pass(kept, grad):
    return (grad,)

def back_keep(v):
    return (v, None)

def back_low(kept, grad):
    return (low(grad),)
low.defvjp(low_keep, low_pass)
low_back.defvjp(back_keep, back_low)
EPSILON = 1e-06
MASKED = -1e+30

def matmul(left, right):
    return jnp.dot(left, right, precision=lax.Precision.HIGHEST)

def normalize(values, gain, shift):
    center = values - lax.optimization_barrier(jnp.mean(values, -1, keepdims=True))
    spread = lax.optimization_barrier(jnp.mean(center * center, -1, keepdims=True))
    return center * lax.rsqrt(spread + EPSILON) * gain + shift

def layer(values, params, count):
    a_gain, a_shift, w_qkv, q_bias, v_bias, w_out, o_bias, m_gain, m_shift, w_up, u_bias, w_down, d_bias = params
    normed = low(normalize(values, a_gain, a_shift))
    middle = jnp.zeros((D,), jnp.float32)
    qkv = matmul(normed, w_qkv) + jnp.concatenate([q_bias, middle, v_bias])
    qkv = low_back(low(qkv))
    split = qkv.reshape(SLOTS, 3, HEADS, HEAD)
    query_rows, key_rows, value_rows = (split[:, 0], split[:, 1], split[:, 2])
    scores = jnp.einsum('qhe,khe->hqk', query_rows, key_rows, precision=lax.Precision.HIGHEST) * HEAD ** (-0.5)
    live = jnp.arange(SLOTS) < count * PATCHES
    scores = low_back(jnp.where(live[None, None, :], scores, MASKED))
    probs = jax.nn.softmax(scores, axis=-1)
    mixed = jnp.einsum('hqk,khe->qhe', low(probs), value_rows, precision=lax.Precision.HIGHEST).reshape(SLOTS, D)
    mixed = low_back(low(mixed))
    hidden = values + low_back(matmul(mixed, w_out) + o_bias)
    second = low(normalize(hidden, m_gain, m_shift))
    upper = low_back(matmul(second, w_up) + u_bias)
    active = low(jax.nn.gelu(upper, approximate=False))
    return hidden + low_back(matmul(active, w_down) + d_bias)

def reference(tokens, cotangent, views, attn_gain, attn_shift, qkv_weight, query_bias, value_bias, out_weight, out_bias, mlp_gain, mlp_shift, up_weight, up_bias, down_weight, down_bias):
    stacked = (attn_gain, attn_shift, qkv_weight, query_bias, value_bias, out_weight, out_bias, mlp_gain, mlp_shift, up_weight, up_bias, down_weight, down_bias)
    first = tuple((w[0].astype(jnp.float32) for w in stacked))
    second = tuple((w[1].astype(jnp.float32) for w in stacked))
    rows = tokens.reshape(MICRO * SCENES, SLOTS, D)
    cots = cotangent.reshape(MICRO * SCENES, SLOTS, D)
    counts = views.reshape(MICRO * SCENES)

    def scene(carry, item):
        inputs, cot, count = item

        def pair(values, bump, prm_a, prm_b):
            y_first = layer(values, prm_a, count)
            carried = low_back(low(y_first) + bump)
            return (y_first, layer(carried, prm_b, count))
        outs, back = jax.vjp(pair, inputs.astype(jnp.float32), jnp.zeros((SLOTS, D), jnp.float32), first, second)
        g_in, g_mid, g_a, g_b = back((jnp.zeros_like(outs[0]), cot.astype(jnp.float32)))
        carry = (jax.tree.map(lambda s, t: s + t, carry[0], g_a), jax.tree.map(lambda s, t: s + t, carry[1], g_b))
        return (carry, (outs[0].astype(jnp.bfloat16), outs[1].astype(jnp.bfloat16), g_in.astype(jnp.bfloat16), g_mid.astype(jnp.bfloat16)))
    init = (jax.tree.map(jnp.zeros_like, first), jax.tree.map(jnp.zeros_like, second))
    (grad_a, grad_b), (y_a, y_b, g_in, g_mid) = lax.scan(scene, init, (rows, cots, counts))
    shaped = (MICRO, SCENES, SLOTS, D)
    layer_out = jnp.stack([y_a.reshape(shaped), y_b.reshape(shaped)])
    input_grads = jnp.stack([g_in.reshape(shaped), g_mid.reshape(shaped)])
    grads = tuple((jnp.stack([left, right]) for left, right in zip(grad_a, grad_b)))
    return (layer_out, input_grads, grads[0], grads[1], grads[2], grads[3], grads[4], grads[5], grads[6], grads[7], grads[8], grads[9], grads[10], grads[11], grads[12])
```

```python
import jax
import jax.numpy as jnp
from jax import lax
from jax.experimental import pallas as pl
from jax.experimental.pallas import tpu as pltpu
from jax.sharding import PartitionSpec as P

HEADS = 6
HEAD = 64
PATCHES = 64
EPSILON = 1e-06
MASKED = -1e30
LANES = 128
CUTS = 16
F32 = jnp.float32
BF16 = jnp.bfloat16
VMEM_LIMIT = 60 * 2**20
def dot(a, b):
    return lax.dot_general(a, b, (((1,), (0,)), ((), ())), preferred_element_type=F32)


def dot_nt(a, b):
    return lax.dot_general(a, b, (((1,), (1,)), ((), ())), preferred_element_type=F32)


def unit_rows(values):
    center = values - jnp.mean(values, -1, keepdims=True)
    spread = jnp.mean(center * center, -1, keepdims=True)
    scale = lax.rsqrt(spread + EPSILON)
    return center * scale, scale


def row(vec_ref, i):
    return vec_ref[i : i + 1, :]


A_GAIN, A_SHIFT, Q_BIAS, V_BIAS, O_BIAS, M_GAIN, M_SHIFT, D_BIAS = range(8)


def forward(x, count, vec, ub, w, r, wait, done):
    slots, width = x.shape
    ff = ub.shape[1]
    unit, _ = unit_rows(x)
    r["a"][...] = (unit * row(vec, A_GAIN) + row(vec, A_SHIFT)).astype(BF16)
    done("a")
    wait("qkv")
    a = r["a"][...]
    q = dot(a, w["qkv"][:, :width]) + row(vec, Q_BIAS)
    r["qt"][...] = (q * HEAD**-0.5).astype(BF16).T
    k = dot(a, w["qkv"][:, width : 2 * width]).astype(BF16)
    r["k"][...] = k
    r["kt"][...] = k.T
    v = (dot(a, w["qkv"][:, 2 * width :]) + row(vec, V_BIAS)).astype(BF16)
    r["v"][...] = v
    r["vt"][...] = v.T
    for n in ("qt", "k", "kt", "v"):
        done(n)
    zero = jnp.zeros((HEAD, slots), BF16)
    groups = slots // PATCHES
    shift = [jnp.where(g < count, 0.0, MASKED).astype(F32) for g in range(groups)]
    for h in range(HEADS):
        pair = slice(h // 2 * 2 * HEAD, (h // 2 * 2 + 2) * HEAD)
        rows = slice(h * HEAD, (h + 1) * HEAD)
        q = r["qt"][rows, :]
        q = jnp.concatenate([q, zero] if h % 2 == 0 else [zero, q], 0)
        s_ref = r["s"].at[h % 2]
        s_ref[...] = dot(r["k"][:, pair], q)
        for c in range(slots // LANES):
            cols = slice(c * LANES, (c + 1) * LANES)
            peak = s_ref[0:PATCHES, cols]
            for g in range(1, groups):
                block = s_ref[g * PATCHES : (g + 1) * PATCHES, cols]
                peak = jnp.maximum(peak, block if g < 2 else block + shift[g])
            peak = jnp.max(peak, 0, keepdims=True)
            total = jnp.zeros((1, LANES), F32)
            acc = jnp.zeros((PATCHES, LANES), F32)
            for g in range(groups):
                block = s_ref[g * PATCHES : (g + 1) * PATCHES, cols]
                e = jnp.exp(block - (peak - shift[g]))
                acc = acc + e
                r["e"][h, g * PATCHES : (g + 1) * PATCHES, cols] = e.astype(BF16)
            total = jnp.sum(acc, 0, keepdims=True)
            r["inv"][h : h + 1, cols] = 1.0 / total
        o = dot(r["vt"][rows, :], r["e"][h]) * r["inv"][h : h + 1, :]
        r["ot"][rows, :] = o
    done("e")
    done("inv")
    done("ot")
    wait("out")
    o = r["ot"][...].astype(BF16).T
    hidden = x + dot(o, w["out"][...]) + row(vec, O_BIAS)
    r["h"][...] = hidden
    done("h")
    unit, _ = unit_rows(hidden)
    r["c"][...] = (unit * row(vec, M_GAIN) + row(vec, M_SHIFT)).astype(BF16)
    done("c")
    wait("up")
    c = r["c"][...]
    step = 256
    for f in range(0, ff, step):
        cols = slice(f, f + step)
        u = dot(c, w["up"][:, cols]) + ub[:, cols]
        phi = 0.5 + 0.5 * lax.erf(u * 0.5**0.5)
        density = jnp.exp(-0.5 * u * u) * 0.3989422804014327
        r["z"][:, cols] = (u * phi).astype(BF16)
        r["gp"][:, cols] = (phi + u * density).astype(BF16)
    done("z")
    done("gp")
    wait("down")
    return hidden + dot(r["z"][...], w["down"][...]) + row(vec, D_BIAS)


def nothing(name):
    pass


def sizes(slots, width, ff):
    return dict(
        a=((slots, width), BF16),
        qt=((width, slots), BF16),
        k=((slots, width), BF16),
        kt=((width, slots), BF16),
        v=((slots, width), BF16),
        vt=((width, slots), BF16),
        s=((2, slots, slots), F32),
        e=((HEADS, slots, slots), BF16),
        inv=((8, slots), F32),
        ot=((width, slots), F32),
        h=((slots, width), F32),
        c=((slots, width), BF16),
        z=((slots, ff), BF16),
        gp=((slots, ff), BF16),
    )


def norm_back(grad, gain, unit, scale):
    t = grad * gain
    inner = jnp.mean(t, -1, keepdims=True)
    along = jnp.mean(t * unit, -1, keepdims=True)
    return scale * (t - inner - unit * along)


M_GAIN_G, M_SHIFT_G, A_GAIN_G, A_SHIFT_G = range(4)


def backward_mlp(grad, vec, w, r, wait, done):
    slots, width = grad.shape
    ff = r["du"].shape[1]
    low = grad.astype(BF16)
    step = 256
    for f in range(0, ff, step):
        cols = slice(f, f + step)
        dz = dot_nt(low, w["down"][cols, :])
        r["du"][:, cols] = (dz * r["gp"][:, cols].astype(F32)).astype(BF16)
    done("du")
    dc = dot_nt(r["du"][...], w["up"][...])
    unit, scale = unit_rows(r["h"][...])
    r["small"][M_GAIN_G : M_GAIN_G + 1, :] = jnp.sum(dc * unit, 0, keepdims=True)
    r["small"][M_SHIFT_G : M_SHIFT_G + 1, :] = jnp.sum(dc, 0, keepdims=True)
    dh = grad + norm_back(dc, row(vec, M_GAIN), unit, scale)
    r["dh"][...] = dh
    r["dp"][...] = dh.astype(BF16)
    done("dp")


def backward_attention(x, vec, w, r, done):
    slots, width = x.shape
    dot_t = dot_nt(w["out"][...], r["dp"][...])
    r["dot"][...] = dot_t
    zero = jnp.zeros((HEAD, slots), BF16)
    for h in range(HEADS):
        pair = slice(h // 2 * 2 * HEAD, (h // 2 * 2 + 2) * HEAD)
        rows = slice(h * HEAD, (h + 1) * HEAD)
        g = (r["dot"][rows, :] * r["inv"][h : h + 1, :]).astype(BF16)
        center = jnp.sum(g.astype(F32) * r["ot"][rows, :], 0, keepdims=True)
        wide = jnp.concatenate([g, zero] if h % 2 == 0 else [zero, g], 0)
        s_ref = r["s"].at[h % 2]
        s_ref[...] = dot(r["v"][:, pair], wide)
        for c in range(slots // LANES):
            cols = slice(c * LANES, (c + 1) * LANES)
            for b in range(0, slots, PATCHES):
                block = s_ref[b : b + PATCHES, cols] - center[:, cols]
                r["ds"][h % 2, b : b + PATCHES, cols] = (
                    block * r["e"][h, b : b + PATCHES, cols].astype(F32)
                ).astype(BF16)
        ds = r["ds"][h % 2]
        dq = dot(r["kt"][rows, :], ds) * HEAD**-0.5
        dk = dot_nt(r["qt"][rows, :], ds)
        dv = dot_nt(g, r["e"][h])
        r["dqkv"][rows, :] = dq.astype(BF16)
        r["dqkv"][width + h * HEAD : width + (h + 1) * HEAD, :] = dk.astype(BF16)
        r["dqkv"][2 * width + h * HEAD : 2 * width + (h + 1) * HEAD, :] = dv.astype(BF16)
    done("dqkv")
    da = dot(w["qkv"][...], r["dqkv"][...]).T
    unit, scale = unit_rows(x)
    r["small"][A_GAIN_G : A_GAIN_G + 1, :] = jnp.sum(da * unit, 0, keepdims=True)
    r["small"][A_SHIFT_G : A_SHIFT_G + 1, :] = jnp.sum(da, 0, keepdims=True)
    done("small")
    return r["dh"][...] + norm_back(da, row(vec, A_GAIN), unit, scale)


def back_sizes(slots, width, ff):
    return dict(
        du=((slots, ff), BF16),
        dh=((slots, width), F32),
        dp=((slots, width), BF16),
        dot=((width, slots), F32),
        ds=((2, slots, slots), BF16),
        dqkv=((3 * width, slots), BF16),
        small=((8, width), F32),
    )


SAVED = ("a", "qt", "kt", "v", "e", "inv", "ot", "h", "c", "z", "gp")
TERMS = ("a", "ot", "c", "z", "du", "dp", "dqkv", "small")
WEIGHTS = ("qkv", "out", "up", "down")


def run(body, ins, outs, scratch, aliases=None):
    space = {"s": pltpu.SMEM, "v": pltpu.VMEM, "a": pl.ANY}
    return pl.pallas_call(
        body,
        out_shape=[jax.ShapeDtypeStruct(s, t) for s, t, _ in outs],
        in_specs=[pl.BlockSpec(memory_space=space[k]) for _, k in ins],
        out_specs=[pl.BlockSpec(memory_space=space[k]) for _, _, k in outs],
        scratch_shapes=scratch,
        input_output_aliases=aliases or {},
        compiler_params=pltpu.CompilerParams(vmem_limit_bytes=VMEM_LIMIT),
    )(*[x for x, _ in ins])


class Moves:
    def __init__(self, sem):
        self.sem = sem
        self.made = {}
        self.open = []

    def start(self, name, src, dst):
        copy = pltpu.make_async_copy(src, dst, self.sem.at[len(self.made)])
        copy.start()
        self.made[name] = copy
        self.open.append(name)

    def wait(self, name):
        if name in self.open:
            self.made[name].wait()
            self.open.remove(name)

    def finish(self):
        for name in list(self.open):
            self.wait(name)


def forward_step(info, slot, tokens, old, vec, ub, weights, dims):
    slots, width, ff = dims
    shapes = sizes(*dims)
    wshapes = weight_sizes(width, ff)
    names = list(shapes)
    n_in = 8 + (old is not None)

    def body(*refs):
        info_ref, x_ref, vec_ref, ub_ref = refs[:4]
        w_hbm = dict(zip(WEIGHTS, refs[4:8]))
        y_hbm, all_hbm = refs[n_in : n_in + 2]
        saved = dict(zip(SAVED, refs[n_in + 2 : n_in + 2 + len(SAVED)]))
        rest = refs[n_in + 2 + len(SAVED) :]
        w = dict(zip(WEIGHTS, rest[:4]))
        r = dict(zip(names, rest[4 : 4 + len(names)]))
        y, sem = rest[4 + len(names) :]

        @pl.when(info_ref[0] == 0)
        def _():
            moves = Moves(sem)
            for n in WEIGHTS:
                moves.start(n, w_hbm[n].at[0], w[n])

            def done(n):
                if n in saved:
                    moves.start("save " + n, r[n], saved[n])

            result = forward(
                x_ref[...].astype(F32), info_ref[2 + slot], vec_ref, ub_ref, w, r, moves.wait, done
            )
            y[...] = result.astype(BF16)
            moves.start("y", y, y_hbm)
            moves.start("all", y, all_hbm.at[slot])
            moves.finish()

    ins = [(info, "s"), (tokens, "v"), (vec, "v"), (ub, "v")] + [(w, "a") for w in weights]
    if old is not None:
        ins.append((old, "a"))
    outs = [((slots, width), BF16, "a"), ((2, slots, width), BF16, "a")]
    outs += [(*shapes[n], "a") for n in SAVED]
    scratch = [pltpu.VMEM(wshapes[n], BF16) for n in WEIGHTS]
    scratch += [pltpu.VMEM(*shapes[n]) for n in names]
    scratch += [pltpu.VMEM((slots, width), BF16), pltpu.SemaphoreType.DMA((len(SAVED) + 6,))]
    got = run(body, ins, outs, scratch, {8: 1} if old is not None else None)
    return got[0], got[1], dict(zip(SAVED, got[2:]))


def weight_sizes(width, ff):
    return dict(qkv=(width, 3 * width), out=(width, width), up=(width, ff), down=(ff, width))


def both_step(info, slot, inputs, cotangent, outs_old, grads_old, saved, vec, ub, weights, dims):
    slots, width, ff = dims
    shapes = {**sizes(*dims), **back_sizes(*dims)}
    wshapes = weight_sizes(width, ff)
    names = list(shapes)
    kept = ("a", "ot", "c", "z")
    first = grads_old is None
    n_in = 14 if first else 15
    back = ("du", "dp", "dqkv", "small")

    def body(*refs):
        info_ref, x_ref, cot_ref, vec_ref, ub_ref = refs[:5]
        w_hbm = dict(zip(WEIGHTS, refs[5:9]))
        rest = refs[n_in:]
        all_hbm, grads_hbm, g_hbm = rest[:3]
        saved_hbm = dict(zip(kept + back, rest[3:11]))
        rest = rest[11:]
        w = dict(zip(WEIGHTS, rest[:4]))
        r = dict(zip(names, rest[4 : 4 + len(names)]))
        y, g, sem = rest[4 + len(names) :]

        @pl.when(info_ref[0] == 1)
        def _():
            moves = Moves(sem)
            for n in WEIGHTS:
                moves.start(n, w_hbm[n].at[0], w[n])

            def done(n):
                if n in saved_hbm:
                    moves.start("save " + n, r[n], saved_hbm[n])

            x = x_ref[...].astype(F32)
            result = forward(x, info_ref[2 + slot], vec_ref, ub_ref, w, r, moves.wait, done)
            y[...] = result.astype(BF16)
            moves.start("y", y, all_hbm.at[slot])
            backward_mlp(cot_ref[...].astype(F32), vec_ref, w, r, moves.wait, done)
            g[...] = backward_attention(x_ref[...].astype(F32), vec_ref, w, r, done).astype(BF16)
            moves.start("g", g, g_hbm)
            moves.start("grads", g, grads_hbm.at[slot])
            moves.finish()

    ins = [(info, "s"), (inputs, "v"), (cotangent, "v"), (vec, "v"), (ub, "v")]
    ins += [(w, "a") for w in weights]
    ins += [(outs_old, "a")] + [(saved[n], "a") for n in kept]
    aliases = {9: 0}
    for i in range(4):
        aliases[10 + i] = 3 + i
    if not first:
        ins.append((grads_old, "a"))
        aliases[14] = 1
    outs = [((2, slots, width), BF16, "a")] * 2 + [((slots, width), BF16, "a")]
    outs += [(*shapes[n], "a") for n in kept + back]
    scratch = [pltpu.VMEM(wshapes[n], BF16) for n in WEIGHTS]
    scratch += [pltpu.VMEM(*shapes[n]) for n in names]
    scratch += [pltpu.VMEM((slots, width), BF16)] * 2 + [pltpu.SemaphoreType.DMA((15,))]
    got = run(body, ins, outs, scratch, aliases)
    return got[0], got[1], got[2], dict(saved, **dict(zip(kept + back, got[3:])))


def back_step(info, slot, inputs, grad, grads_old, saved, terms, vec, weights, dims):
    slots, width, ff = dims
    shapes = {**sizes(*dims), **back_sizes(*dims)}
    wshapes = weight_sizes(width, ff)
    names = [n for n in shapes if n not in ("a", "k", "vt", "c", "z")]
    loads = ("gp", "h", "inv", "ot", "v", "e", "kt", "qt")
    back = ("du", "dp", "dqkv", "small")
    n_in = 8 + len(loads) + 5

    def body(*refs):
        info_ref, x_ref, grad_ref, vec_ref = refs[:4]
        w_hbm = dict(zip(WEIGHTS, refs[4:8]))
        saved_hbm = dict(zip(loads, refs[8 : 8 + len(loads)]))
        rest = refs[n_in:]
        grads_hbm = rest[0]
        out_hbm = dict(zip(back, rest[1:5]))
        rest = rest[5:]
        w = dict(zip(WEIGHTS, rest[:4]))
        r = dict(zip(names, rest[4 : 4 + len(names)]))
        g, sem = rest[4 + len(names) :]

        @pl.when(info_ref[0] == 0)
        def _():
            moves = Moves(sem)
            for n in ("down", "gp", "up", "h", "out", "inv", "ot", "v", "e", "kt", "qt", "qkv"):
                if n in w:
                    moves.start(n, w_hbm[n].at[0], w[n])
                else:
                    moves.start(n, saved_hbm[n], r[n])

            def done(n):
                if n in out_hbm:
                    moves.start("save " + n, r[n], out_hbm[n])

            for n in ("down", "gp", "up", "h"):
                moves.wait(n)
            backward_mlp(grad_ref[...].astype(F32), vec_ref, w, r, moves.wait, done)
            for n in ("out", "inv", "ot", "v", "e", "kt", "qt", "qkv"):
                moves.wait(n)
            g[...] = backward_attention(x_ref[...].astype(F32), vec_ref, w, r, done).astype(BF16)
            moves.start("grads", g, grads_hbm.at[slot])
            moves.finish()

    ins = [(info, "s"), (inputs, "v"), (grad, "v"), (vec, "v")]
    ins += [(w, "a") for w in weights] + [(saved[n], "a") for n in loads]
    ins += [(grads_old, "a")] + [(terms[n], "a") for n in back]
    base = 8 + len(loads)
    aliases = {base + i: i for i in range(5)}
    outs = [((2, slots, width), BF16, "a")] + [(*shapes[n], "a") for n in back]
    scratch = [pltpu.VMEM(wshapes[n], BF16) for n in WEIGHTS]
    scratch += [pltpu.VMEM(*shapes[n]) for n in names]
    scratch += [pltpu.VMEM((slots, width), BF16), pltpu.SemaphoreType.DMA((20,))]
    got = run(body, ins, outs, scratch, aliases)
    return got[0], dict(terms, **dict(zip(back, got[1:])))


def scatter_blocks(moves, me, blocks, keep_hbm, send_hbm):
    for p in range(CUTS):
        place = jnp.bitwise_xor(p, me)

        @pl.when(jnp.bitwise_and(place, 1) == 0)
        def _():
            pltpu.make_async_copy(blocks.at[p], keep_hbm.at[place // 2], moves.sem.at[p]).start()

        @pl.when(jnp.bitwise_and(place, 1) == 1)
        def _():
            pltpu.make_async_copy(blocks.at[p], send_hbm.at[place // 2], moves.sem.at[p]).start()

    for p in range(CUTS):
        pltpu.make_async_copy(blocks.at[p], keep_hbm.at[0], moves.sem.at[p]).wait()


def down_grads(info, terms, grads, cots, dims):
    slots, width, ff = dims
    deep = ff // CUTS

    def body(info_ref, z0, z1, g0, g1, c0, c1, keep, send, sums, z, m, blocks, sem, sem2):
        moves = Moves(sem)
        halves = (slice(0, slots), slice(slots, 2 * slots))
        moves.start("z0", z0, z.at[halves[0]])
        moves.start("z1", z1, z.at[halves[1]])

        @pl.when(info_ref[0] == 0)
        def _():
            m[halves[0], :] = g0[...]
            m[halves[1], :] = g1[...]

        @pl.when(info_ref[0] == 1)
        def _():
            m[halves[0], :] = c0[...]
            m[halves[1], :] = c1[...]

        moves.finish()
        ones = jnp.ones((16, 2 * slots), BF16)
        sums[...] = dot(ones, m[...])[:8]
        for j in range(4):
            part = dot(z[:, j * 4 * deep : (j + 1) * 4 * deep].T, m[...]).astype(BF16)
            blocks[4 * j : 4 * j + 4] = part.reshape(4, deep, width)
        scatter_blocks(Moves(sem2), info_ref[1], blocks, keep, send)

    ins = [(info, "s"), (terms[0]["z"], "a"), (terms[1]["z"], "a")]
    ins += [(x, "v") for x in (*grads, *cots)]
    half = ((CUTS // 2, deep, width), BF16, "a")
    scratch = [
        pltpu.VMEM((2 * slots, ff), BF16),
        pltpu.VMEM((2 * slots, width), BF16),
        pltpu.VMEM((CUTS, deep, width), BF16),
        pltpu.SemaphoreType.DMA((2,)),
        pltpu.SemaphoreType.DMA((CUTS,)),
    ]
    return run(body, ins, [half, half, ((8, width), F32, "v")], scratch)


def up_grads(info, terms, dims):
    slots, width, ff = dims
    deep = width // 4

    def body(info_ref, c0, c1, d0, d1, keep, send, sums, c, d, blocks, sem, sem2):
        moves = Moves(sem)
        halves = (slice(0, slots), slice(slots, 2 * slots))
        moves.start("c0", c0, c.at[halves[0]])
        moves.start("c1", c1, c.at[halves[1]])
        moves.start("d0", d0, d.at[halves[0]])
        moves.start("d1", d1, d.at[halves[1]])
        moves.finish()
        ones = jnp.ones((16, 2 * slots), BF16)
        turned = c[...].T
        for j in range(4):
            cols = slice(j * width, (j + 1) * width)
            sums[j] = dot(ones, d[:, cols])[:8]
            part = dot(turned, d[:, cols]).astype(BF16)
            blocks[4 * j : 4 * j + 4] = part.reshape(4, deep, width)
        scatter_blocks(Moves(sem2), info_ref[1], blocks, keep, send)

    ins = [(info, "s")] + [(terms[m][n], "a") for n in ("c", "du") for m in (0, 1)]
    half = ((CUTS // 2, deep, width), BF16, "a")
    scratch = [
        pltpu.VMEM((2 * slots, width), BF16),
        pltpu.VMEM((2 * slots, ff), BF16),
        pltpu.VMEM((CUTS, deep, width), BF16),
        pltpu.SemaphoreType.DMA((4,)),
        pltpu.SemaphoreType.DMA((CUTS,)),
    ]
    return run(body, ins, [half, half, ((4, 8, width), F32, "v")], scratch)


def attention_grads(info, terms, down_sums, up_sums, dims):
    slots, width, ff = dims
    deep = width // 4
    tall = deep + 16

    def body(
        info_ref, a0, a1, d0, d1, o0, o1, p0, p1, s0, s1, ds_ref, us_ref,
        keep, send, a, d, o, p, blocks, sem, sem2,
    ):
        moves = Moves(sem)
        halves = (slice(0, slots), slice(slots, 2 * slots))
        for m, (x, y, t, u) in enumerate(((a0, d0, o0, p0), (a1, d1, o1, p1))):
            moves.start("a%d" % m, x, a.at[halves[m]])
            moves.start("d%d" % m, y, d.at[m])
            moves.start("o%d" % m, t, o.at[m])
            moves.start("p%d" % m, u, p.at[halves[m]])
        moves.finish()
        ones = jnp.ones((16, slots), BF16)
        wide = jnp.ones((16, 2 * slots), BF16)
        turned = [a[h, :].T for h in halves]
        both = s0[...] + s1[...]
        rows = [
            both[A_GAIN_G : A_GAIN_G + 1], both[A_SHIFT_G : A_SHIFT_G + 1], None, None,
            dot(wide, p[...])[:1], both[M_GAIN_G : M_GAIN_G + 1], both[M_SHIFT_G : M_SHIFT_G + 1],
            ds_ref[:1], us_ref[0, :1], us_ref[1, :1], us_ref[2, :1], us_ref[3, :1],
        ]
        for j in range(3):
            parts = [d[m, j * width : (j + 1) * width, :] for m in (0, 1)]
            if j != 1:
                rows[2 + j // 2] = (dot_nt(ones, parts[0]) + dot_nt(ones, parts[1]))[:1]
            part = (dot_nt(turned[0], parts[0]) + dot_nt(turned[1], parts[1])).astype(BF16)
            blocks[4 * j : 4 * j + 4, :deep] = part.reshape(4, deep, width)
        part = dot(o[0].astype(BF16), p[halves[0], :]) + dot(o[1].astype(BF16), p[halves[1], :])
        blocks[12:16, :deep] = part.astype(BF16).reshape(4, deep, width)
        for i in range(CUTS):
            line = rows[i] if i < 12 else jnp.zeros((1, width), F32)
            blocks[i, deep:] = jnp.broadcast_to(line, (16, width)).astype(BF16)
        scatter_blocks(Moves(sem2), info_ref[1], blocks, keep, send)

    ins = [(info, "s")]
    ins += [(terms[m][n], "a") for n in ("a", "dqkv", "ot", "dp") for m in (0, 1)]
    ins += [(terms[0]["small"], "v"), (terms[1]["small"], "v"), (down_sums, "v"), (up_sums, "v")]
    half = ((CUTS // 2, tall, width), BF16, "a")
    scratch = [
        pltpu.VMEM((2 * slots, width), BF16),
        pltpu.VMEM((2, 3 * width, slots), BF16),
        pltpu.VMEM((2, width, slots), F32),
        pltpu.VMEM((2 * slots, width), BF16),
        pltpu.VMEM((CUTS, tall, width), BF16),
        pltpu.SemaphoreType.DMA((8,)),
        pltpu.SemaphoreType.DMA((CUTS,)),
    ]
    return run(body, ins, [half, half], scratch)


def block(info_ref, own, other, p):
    place = jnp.bitwise_xor(p, info_ref[1])
    mine = own[place // 2]
    theirs = other[place // 2]
    odd = jnp.bitwise_and(place, 1)
    return jnp.where(odd == 1, theirs, mine).astype(F32)


def down_out(info, own, other, dims):
    slots, width, ff = dims
    deep = ff // CUTS

    def body(info_ref, own_ref, other_ref, out):
        for p in range(CUTS):
            out[0, p * deep : (p + 1) * deep, :] = block(info_ref, own_ref, other_ref, p)

    ins = [(info, "s"), (own, "v"), (other, "v")]
    return run(body, ins, [((1, ff, width), F32, "v")], [])[0]


def up_out(info, own, other, dims):
    slots, width, ff = dims
    deep = width // 4

    def body(info_ref, own_ref, other_ref, out):
        for p in range(CUTS):
            j, i = p // 4, p % 4
            out[0, i * deep : (i + 1) * deep, j * width : (j + 1) * width] = block(
                info_ref, own_ref, other_ref, p
            )

    ins = [(info, "s"), (own, "v"), (other, "v")]
    return run(body, ins, [((1, width, ff), F32, "v")], [])[0]


def attention_out(info, own, other, dims):
    slots, width, ff = dims
    deep = width // 4

    def body(info_ref, own_ref, other_ref, qkv, out, *lines):
        for p in range(CUTS):
            j, i = p // 4, p % 4
            got = block(info_ref, own_ref, other_ref, p)
            if j < 3:
                qkv[0, i * deep : (i + 1) * deep, j * width : (j + 1) * width] = got[:deep]
            else:
                out[0, i * deep : (i + 1) * deep, :] = got[:deep]
            if p < 8:
                lines[p][...] = got[deep : deep + 1]
            elif p < 12:
                lines[8][:, (p - 8) * width : (p - 7) * width] = got[deep : deep + 1]

    ins = [(info, "s"), (own, "v"), (other, "v")]
    outs = [((1, width, 3 * width), F32, "v"), ((1, width, width), F32, "v")]
    outs += [((1, width), F32, "v")] * 8 + [((1, ff), F32, "v")]
    return run(body, ins, outs, [])


def swapped(x, bits):
    return lax.ppermute(x, "dp", [(i, i ^ bits) for i in range(CUTS)])


def added(*parts):
    total = parts[0].astype(F32)
    for x in parts[1:]:
        total = total + x.astype(F32)
    return total.astype(BF16)


def all_reduced(keep, send):
    if lax.axis_size("dp") != CUTS:
        return lax.psum(keep, "dp"), lax.psum(send, "dp")
    u = added(keep, swapped(send, 1))
    u = u.reshape(4, 2, *u.shape[1:])
    u = added(u[:, 0], swapped(u[:, 1], 2))
    u = added(u[0], *[swapped(u[j], 4 * j) for j in (1, 2, 3)])
    u = jnp.stack([u] + [swapped(u, 4 * j) for j in (1, 2, 3)])
    u = jnp.stack([u, swapped(u, 2)], 1)
    u = u.reshape(8, *u.shape[2:])
    return u, swapped(u, 1)


def shards(
    tokens, cotangent, views, attn_gain, attn_shift, qkv_weight, query_bias, value_bias,
    out_weight, out_bias, mlp_gain, mlp_shift, up_weight, up_bias, down_weight, down_bias,
):
    dims = (tokens.shape[2], tokens.shape[3], up_bias.shape[1])
    weights = (qkv_weight, out_weight, up_weight, down_weight)
    vec = jnp.concatenate(
        [attn_gain, attn_shift, query_bias, value_bias, out_bias, mlp_gain, mlp_shift, down_bias], 0
    ).astype(F32)
    ub = up_bias.astype(F32)
    section = lax.axis_index("section")
    me = lax.axis_index("dp") if lax.axis_size("dp") == CUTS else jnp.int32(0)
    info = jnp.stack([section, me, views[0, 0], views[1, 0]]).astype(jnp.int32)
    forth = [(0, 1)]
    y0, outs, r0 = forward_step(info, 0, tokens[0, 0], None, vec, ub, weights, dims)
    x0 = lax.ppermute(y0, "section", forth)
    y1, outs, r1 = forward_step(info, 1, tokens[1, 0], outs, vec, ub, weights, dims)
    x1 = lax.ppermute(y1, "section", forth)
    cots = (cotangent[0, 0], cotangent[1, 0])
    outs, grads, g0, t0 = both_step(info, 0, x0, cots[0], outs, None, r0, vec, ub, weights, dims)
    h0 = lax.ppermute(g0, "section", [(1, 0)])
    outs, grads, g1, t1 = both_step(info, 1, x1, cots[1], outs, grads, r1, vec, ub, weights, dims)
    grads, t0 = back_step(info, 0, tokens[0, 0], h0, grads, r0, t0, vec, weights, dims)
    g1, grads = lax.optimization_barrier((g1, grads))
    h1 = lax.ppermute(g1, "section", [(1, 0)])
    keep, send, down_sums = down_grads(info, (t0, t1), (h0, h1), cots, dims)
    down_sum = all_reduced(keep, send)
    grads, t1 = back_step(info, 1, tokens[1, 0], h1, grads, r1, t1, vec, weights, dims)
    keep, send, up_sums = up_grads(info, (t0, t1), dims)
    up_sum = all_reduced(keep, send)
    keep, send = attention_grads(info, (t0, t1), down_sums, up_sums, dims)
    attention_sum = all_reduced(keep, send)
    g_down = down_out(info, *down_sum, dims)
    g_up = up_out(info, *up_sum, dims)
    g_qkv, g_out, *lines = attention_out(info, *attention_sum, dims)
    g_ag, g_as, g_qb, g_vb, g_ob, g_mg, g_ms, g_db, g_ub = lines
    return (
        outs[None, :, None], grads[None, :, None], g_ag, g_as, g_qkv, g_qb, g_vb, g_out, g_ob,
        g_mg, g_ms, g_up, g_ub, g_down, g_db,
    )


def solution(mesh):
    scene = P(None, "dp", None, None)
    line = P("section", None)
    table = P("section", None, None)
    kept = P("section", None, "dp", None, None)
    kinds = (line, line, table, line, line, table, line, line, line, table, line, table, line)
    return jax.shard_map(
        shards,
        mesh=mesh,
        in_specs=(scene, scene, P(None, "dp")) + kinds,
        out_specs=(kept, kept) + kinds,
        check_vma=False,
    )
```

```python
import jax
import jax.numpy as jnp
from jax import lax
from jax.experimental import pallas as pl
from jax.experimental.pallas import tpu as pltpu
from jax.sharding import PartitionSpec as P

HEADS = 6
HEAD = 64
PATCHES = 64
EPSILON = 1e-06
MASKED = -1e30
LANES = 128
CUTS = 16
F32 = jnp.float32
BF16 = jnp.bfloat16
VMEM_LIMIT = 28 * 2**20


def dot(a, b):
    return lax.dot_general(a, b, (((1,), (0,)), ((), ())), preferred_element_type=F32)


def dot_nt(a, b):
    return lax.dot_general(a, b, (((1,), (1,)), ((), ())), preferred_element_type=F32)


def unit_rows(values):
    center = values - jnp.mean(values, -1, keepdims=True)
    spread = jnp.mean(center * center, -1, keepdims=True)
    scale = lax.rsqrt(spread + EPSILON)
    return center * scale, scale


def row(vec, name):
    return vec[name][...].astype(F32)


LINES = ("ag", "as", "qb", "vb", "ob", "mg", "ms", "db", "ub")
CHUNK = 256


def padded(rows, odd):
    zero = jnp.zeros_like(rows)
    return jnp.concatenate([zero, rows] if odd else [rows, zero], 0)


def forward(x_ref, y_ref, count, vec, w, r, wait, done):
    slots, width = x_ref.shape
    ub = row(vec, "ub")
    ff = ub.shape[1]

    unit, _ = unit_rows(x_ref[...].astype(F32))
    a = (unit * row(vec, "ag") + row(vec, "as")).astype(BF16)
    r["a"][...] = a
    wait("qkv")
    q = dot(a, w["qkv"][:, :width]) + row(vec, "qb")
    r["qt"][...] = (q * HEAD**-0.5).astype(BF16).T.reshape(HEADS, HEAD, slots)
    k = dot(a, w["qkv"][:, width : 2 * width]).astype(BF16)
    r["kt"][...] = k.T.reshape(HEADS, HEAD, slots)
    v = (dot(a, w["qkv"][:, 2 * width :]) + row(vec, "vb")).astype(BF16)
    r["vt"][...] = v.T.reshape(HEADS, HEAD, slots)
    for p in range(HEADS // 2):
        r["k"][p] = k[:, p * 2 * HEAD : (p + 1) * 2 * HEAD]
        r["v"][p] = v[:, p * 2 * HEAD : (p + 1) * 2 * HEAD]
    for n in ("a", "qt", "k", "kt", "v"):
        done(n)
    groups = slots // PATCHES
    shift = [jnp.where(g < count, 0.0, MASKED).astype(F32) for g in range(groups)]

    last = HEADS - 1

    def scores(h, odd):
        r["s"][odd] = dot(r["k"][h // 2], padded(r["qt"][h], odd))

    def soften(h, odd):
        s_ref = r["s"].at[odd]
        for c in range(slots // LANES):
            cols = slice(c * LANES, (c + 1) * LANES)
            peak = s_ref[0:PATCHES, cols]
            for g in range(1, groups):
                block = s_ref[g * PATCHES : (g + 1) * PATCHES, cols]
                peak = jnp.maximum(peak, block if g < 2 else block + shift[g])
            peak = jnp.max(peak, 0, keepdims=True)
            acc = jnp.zeros((PATCHES, LANES), F32)
            for g in range(groups):
                block = s_ref[g * PATCHES : (g + 1) * PATCHES, cols]
                e = jnp.exp(block - (peak - shift[g]))
                acc = acc + e
                r["e"][h, g * PATCHES : (g + 1) * PATCHES, cols] = e.astype(BF16)
            r["inv"][h, :, cols] = 1.0 / jnp.sum(acc, 0, keepdims=True)

    def mix(h):
        r["ot"][h] = dot(r["vt"][h], r["e"][h]) * r["inv"][h]

    def pair(i):
        h = 2 * i
        scores(h + 1, 1)
        soften(h, 0)
        if h:
            mix(h - 1)
        if h + 2 < HEADS:
            scores(h + 2, 0)
        soften(h + 1, 1)
        mix(h)

    scores(0, 0)
    for i in range(HEADS // 2):
        pair(i)
    mix(last)
    for n in ("e", "inv", "ot"):
        done(n)
    wait("out")
    o = r["ot"][...].reshape(width, slots).astype(BF16).T
    hidden = x_ref[...].astype(F32) + dot(o, w["out"][...]) + row(vec, "ob")
    r["h"][...] = hidden
    done("h")
    unit, _ = unit_rows(hidden)
    c = (unit * row(vec, "mg") + row(vec, "ms")).astype(BF16)
    r["c"][...] = c
    done("c")
    wait("up")
    for f in range(0, ff, CHUNK):
        cols = slice(f, f + CHUNK)
        u = dot(c, w["up"][:, cols]) + ub[:, cols]
        phi = 0.5 + 0.5 * lax.erf(u * 0.5**0.5)
        density = jnp.exp(-0.5 * u * u) * 0.3989422804014327
        r["z"][:, cols] = (u * phi).astype(BF16)
        r["gp"][:, cols] = (phi + u * density).astype(BF16)
    done("z")
    done("gp")
    wait("down")
    y_ref[...] = (r["h"][...] + dot(r["z"][...], w["down"][...]) + row(vec, "db")).astype(BF16)


def nothing(name):
    pass


def sizes(slots, width, ff):
    turned = ((HEADS, HEAD, slots), BF16)
    pairs = ((HEADS // 2, slots, 2 * HEAD), BF16)
    return dict(
        a=((slots, width), BF16),
        qt=turned,
        k=pairs,
        kt=turned,
        v=pairs,
        vt=turned,
        s=((2, slots, slots), F32),
        e=((HEADS, slots, slots), BF16),
        inv=((HEADS, 1, slots), F32),
        ot=((HEADS, HEAD, slots), F32),
        h=((slots, width), F32),
        c=((slots, width), BF16),
        z=((slots, ff), BF16),
        gp=((slots, ff), BF16),
    )


def norm_back(grad, gain, unit, scale):
    t = grad * gain
    inner = jnp.mean(t, -1, keepdims=True)
    along = jnp.mean(t * unit, -1, keepdims=True)
    return scale * (t - inner - unit * along)


M_GAIN_G, M_SHIFT_G, A_GAIN_G, A_SHIFT_G = range(4)


def backward_mlp(grad_ref, vec, w, r, wait, done):
    slots, width = grad_ref.shape
    ff = r["du"].shape[1]
    wait("down")
    wait("gp")
    low = grad_ref[...]
    for f in range(0, ff, CHUNK):
        cols = slice(f, f + CHUNK)
        dz = dot_nt(low, w["down"][cols, :])
        r["du"][:, cols] = (dz * r["gp"][:, cols].astype(F32)).astype(BF16)
    done("du")
    wait("up")
    dc = dot_nt(r["du"][...], w["up"][...])
    wait("h")
    unit, scale = unit_rows(r["h"][...])
    r["small"][M_GAIN_G : M_GAIN_G + 1, :] = jnp.sum(dc * unit, 0, keepdims=True)
    r["small"][M_SHIFT_G : M_SHIFT_G + 1, :] = jnp.sum(dc, 0, keepdims=True)
    dh = low.astype(F32) + norm_back(dc, row(vec, "mg"), unit, scale)
    r["dh"][...] = dh
    r["dp"][...] = dh.astype(BF16)
    done("dp")


def backward_attention(x_ref, g_ref, vec, w, r, wait, done):
    slots, width = x_ref.shape
    wait("out")
    dot_t = dot_nt(w["out"][...], r["dp"][...])
    r["dot"][...] = dot_t.reshape(HEADS, HEAD, slots)

    last = HEADS - 1
    for n in ("inv", "ot", "v", "e", "kt", "qt"):
        wait(n)

    def spread(h, odd):
        g = (r["dot"][h] * r["inv"][h]).astype(BF16)
        r["g"][odd] = g
        r["center"][odd] = jnp.sum(g.astype(F32) * r["ot"][h], 0, keepdims=True)
        r["s"][odd] = dot(r["v"][h // 2], padded(g, odd))

    def weigh(h, odd):
        s_ref = r["s"].at[odd]
        for c in range(slots // LANES):
            cols = slice(c * LANES, (c + 1) * LANES)
            center = r["center"][odd, :, cols]
            for b in range(0, slots, PATCHES):
                block = s_ref[b : b + PATCHES, cols] - center
                r["ds"][odd, b : b + PATCHES, cols] = (
                    block * r["e"][h, b : b + PATCHES, cols].astype(F32)
                ).astype(BF16)

    def gather(h, odd):
        ds = r["ds"][odd]
        r["dqkv"][0, h] = (dot(r["kt"][h], ds) * HEAD**-0.5).astype(BF16)
        r["dqkv"][1, h] = dot_nt(r["qt"][h], ds).astype(BF16)

    def gather_v(h, odd):
        r["dqkv"][2, h] = dot_nt(r["g"][odd], r["e"][h]).astype(BF16)

    def pair(i):
        h = 2 * i
        gather_v(h, 0)
        spread(h + 1, 1)
        weigh(h, 0)
        if h:
            gather(h - 1, 1)
        gather_v(h + 1, 1)
        if h + 2 < HEADS:
            spread(h + 2, 0)
        weigh(h + 1, 1)
        gather(h, 0)

    spread(0, 0)
    for i in range(HEADS // 2):
        pair(i)
    gather(last, 1)
    done("dqkv")

    wait("qkv")
    da = dot(w["qkv"][...], r["dqkv"][...].reshape(3 * width, slots)).T
    unit, scale = unit_rows(x_ref[...].astype(F32))
    r["small"][A_GAIN_G : A_GAIN_G + 1, :] = jnp.sum(da * unit, 0, keepdims=True)
    r["small"][A_SHIFT_G : A_SHIFT_G + 1, :] = jnp.sum(da, 0, keepdims=True)
    done("small")
    g_ref[...] = (r["dh"][...] + norm_back(da, row(vec, "ag"), unit, scale)).astype(BF16)


def back_sizes(slots, width, ff):
    return dict(
        du=((slots, ff), BF16),
        dh=((slots, width), F32),
        dp=((slots, width), BF16),
        dot=((HEADS, HEAD, slots), F32),
        ds=((2, slots, slots), BF16),
        g=((2, HEAD, slots), BF16),
        center=((2, 1, slots), F32),
        dqkv=((3, HEADS, HEAD, slots), BF16),
        small=((8, width), F32),
    )


WEIGHTS = ("qkv", "out", "up", "down")
SAVED = ("a", "qt", "kt", "v", "e", "inv", "ot", "h", "c", "z", "gp")
TERMS = ("du", "dp", "dqkv", "small", "dm")
STEPS = 3


def run(body, ins, outs, scratch, aliases=None, us=1):
    space = {"s": pltpu.SMEM, "v": pltpu.VMEM, "a": pl.ANY}
    return pl.pallas_call(
        body,
        out_shape=[jax.ShapeDtypeStruct(s, t) for s, t, _ in outs],
        in_specs=[pl.BlockSpec(memory_space=space[k]) for _, k in ins],
        out_specs=[pl.BlockSpec(memory_space=space[k]) for _, _, k in outs],
        scratch_shapes=scratch,
        input_output_aliases=aliases or {},
        compiler_params=pltpu.CompilerParams(vmem_limit_bytes=VMEM_LIMIT),
        cost_estimate=pl.CostEstimate(
            flops=us * 10**9, bytes_accessed=us * 2 * 10**6, transcendentals=0
        ),
    )(*[x for x, _ in ins])


def weight_sizes(width, ff):
    return dict(qkv=(width, 3 * width), out=(width, width), up=(width, ff), down=(ff, width))


def all_sizes(dims):
    slots, width, ff = dims
    return {**sizes(*dims), **back_sizes(*dims), "dm": ((slots, width), BF16)}


class Moves:
    def __init__(self, sem):
        self.sem = sem
        self.used = 0
        self.made = {}

    def make(self, name, src, dst):
        self.made[name] = pltpu.make_async_copy(src, dst, self.sem.at[self.used])
        self.used += 1
        return self.made[name]

    def start(self, name, src, dst):
        self.make(name, src, dst).start()

    def wait(self, name):
        if name in self.made:
            self.made.pop(name).wait()

    def finish(self):
        for name in list(self.made):
            self.wait(name)


def blank(dims):
    slots, width, _ = dims
    shapes = all_sizes(dims)
    outs = [((slots, width), BF16, "a")] + [((2, slots, width), BF16, "a")] * 2
    outs += [((2, *shapes[n][0]), shapes[n][1], "a") for n in SAVED + TERMS]

    def body(*refs):
        pass

    got = run(body, [], outs, [])
    return got[0], tuple(got[1:])


def cell(step, views, lines, tokens, cotangent, recv, weights, bufs, dims):
    slots, width, ff = dims
    shapes = all_sizes(dims)
    wshapes = weight_sizes(width, ff)
    names = [n for n in shapes if n != "dm"]
    n_in = 2 + len(lines) + 3 + 4
    loads = ("gp", "h", "inv", "ot", "v", "e", "kt", "qt")

    def body(*refs):
        step_ref, views_ref = refs[:2]
        vec = dict(zip(LINES, refs[2 : 2 + len(lines)]))
        tokens_hbm, cot_hbm, recv_hbm = refs[2 + len(lines) : 5 + len(lines)]
        w_hbm = dict(zip(WEIGHTS, refs[5 + len(lines) : n_in]))
        rest = refs[n_in + len(bufs) :]
        send_hbm, outs_hbm, grads_hbm = rest[:3]
        kept = dict(zip(SAVED + TERMS, rest[3:]))
        rest = rest[3 + len(SAVED + TERMS) :]
        w = dict(zip(WEIGHTS, rest[:4]))
        r = dict(zip(names, rest[4 : 4 + len(names)]))
        x, dm, y, sem = rest[4 + len(names) :]
        moves = Moves(sem)
        t = step_ref[0]
        lead = lax.axis_index("section") == 0
        run_f = jnp.where(lead, t < 2, t > 0)
        run_b = jnp.where(lead, t == 2, t > 0)
        slot = jnp.where(lead, t % 2, jnp.maximum(t - 1, 0))
        only_b = jnp.logical_and(lead, run_b)
        not_lead = jnp.logical_not(lead)
        token_copy = moves.make("x", tokens_hbm.at[slot, 0], x)
        recv_copy = pltpu.make_async_copy(recv_hbm, x, token_copy_sem(moves, "x"))
        cot_copy = moves.make("dm", cot_hbm.at[slot, 0], dm)
        grad_copy = pltpu.make_async_copy(recv_hbm, dm, token_copy_sem(moves, "dm"))
        w_copy = {n: moves.make("w " + n, w_hbm[n].at[0], w[n]) for n in WEIGHTS}
        l_copy = {n: moves.make("l " + n, kept[n].at[slot], r[n]) for n in loads}
        s_copy = {n: moves.make("s " + n, r[n], kept[n].at[slot]) for n in SAVED}
        b_copy = {n: moves.make("b " + n, r[n], kept[n].at[slot]) for n in TERMS[:4]}
        b_copy["dm"] = moves.make("b dm", dm, kept["dm"].at[slot])
        y_copy = moves.make("y", y, outs_hbm.at[slot])
        g_copy = moves.make("g", x, grads_hbm.at[slot])
        y_send = moves.make("ys", y, send_hbm)
        g_send = moves.make("gs", x, send_hbm)

        @pl.when(run_f)
        def _():
            @pl.when(lead)
            def _():
                token_copy.start()

            @pl.when(not_lead)
            def _():
                recv_copy.start()

            for n in WEIGHTS:
                w_copy[n].start()

            @pl.when(not_lead)
            def _():
                cot_copy.start()

            token_copy.wait()
            forward(
                x, y, views_ref[slot, 0], vec, w, r,
                lambda n: w_copy[n].wait(), lambda n: s_copy[n].start() if n in s_copy else None,
            )
            y_copy.start()

            @pl.when(lead)
            def _():
                y_send.start()

            @pl.when(not_lead)
            def _():
                cot_copy.wait()

        @pl.when(only_b)
        def _():
            grad_copy.start()
            for n in ("down", "gp", "up", "h", "out", "inv", "ot", "v", "e", "kt", "qt", "qkv"):
                (w_copy if n in w_copy else l_copy)[n].start()
            token_copy.start()
            grad_copy.wait()
            for n in ("down", "gp", "up", "h"):
                (w_copy if n in w_copy else l_copy)[n].wait()

        @pl.when(run_b)
        def _():
            b_copy["dm"].start()
            backward_mlp(dm, vec, w, r, nothing, lambda n: b_copy[n].start())

            @pl.when(only_b)
            def _():
                for n in ("out", "inv", "ot", "v", "e", "kt", "qt", "qkv"):
                    (w_copy if n in w_copy else l_copy)[n].wait()
                token_copy.wait()

            backward_attention(x, x, vec, w, r, nothing, lambda n: b_copy[n].start())
            g_copy.start()

            @pl.when(not_lead)
            def _():
                g_send.start()

        @pl.when(run_f)
        def _():
            for n in SAVED:
                s_copy[n].wait()
            y_copy.wait()

            @pl.when(lead)
            def _():
                y_send.wait()

        @pl.when(run_b)
        def _():
            for n in TERMS:
                b_copy[n].wait()
            g_copy.wait()

            @pl.when(not_lead)
            def _():
                g_send.wait()

    ins = [(step, "s"), (views, "s")] + [(v, "v") for v in lines]
    ins += [(x, "a") for x in (tokens, cotangent, recv, *weights, *bufs)]
    outs = [((slots, width), BF16, "a")] + [(b.shape, b.dtype, "a") for b in bufs]
    scratch = [pltpu.VMEM(wshapes[n], BF16) for n in WEIGHTS]
    scratch += [pltpu.VMEM(*shapes[n]) for n in names]
    scratch += [pltpu.VMEM((slots, width), BF16)] * 3 + [pltpu.SemaphoreType.DMA((40,))]
    got = run(body, ins, outs, scratch, {n_in + i: 1 + i for i in range(len(bufs))})
    return got[0], tuple(got[1:])


def token_copy_sem(moves, name):
    return moves.sem.at[list(moves.made).index(name)]


def scatter_blocks(sem, me, blocks, keep_hbm, send_hbm):
    for p in range(CUTS):
        place = jnp.bitwise_xor(p, me)

        @pl.when(jnp.bitwise_and(place, 1) == 0)
        def _():
            pltpu.make_async_copy(blocks.at[p], keep_hbm.at[place // 2], sem.at[p]).start()

        @pl.when(jnp.bitwise_and(place, 1) == 1)
        def _():
            pltpu.make_async_copy(blocks.at[p], send_hbm.at[place // 2], sem.at[p]).start()

    for p in range(CUTS):
        pltpu.make_async_copy(blocks.at[p], keep_hbm.at[0], sem.at[p]).wait()


def own_place():
    return lax.axis_index("dp") if lax.axis_size("dp") == CUTS else 0


def down_grads(z, dm, recv, dims):
    slots, width, ff = dims
    deep = width // 4

    def body(z_hbm, dm_hbm, recv_hbm, keep, send, sums, z_ref, m, blocks, sem, sem2):
        moves = Moves(sem)
        lead = lax.axis_index("section") == 0
        moves.start("m0", dm_hbm.at[0], m.at[0])
        first = moves.make("m1", dm_hbm.at[1], m.at[1])
        second = pltpu.make_async_copy(recv_hbm, m.at[1], sem.at[1])

        @pl.when(lead)
        def _():
            second.start()

        @pl.when(jnp.logical_not(lead))
        def _():
            first.start()

        for i in (0, 1):
            moves.start("z%d" % i, z_hbm.at[i], z_ref.at[i])
        moves.wait("m0")
        moves.wait("m1")
        ones = jnp.ones((16, slots), BF16)
        sums[...] = (dot(ones, m[0]) + dot(ones, m[1]))[:8]
        turned = [m[i].T for i in (0, 1)]
        moves.finish()
        for j in range(4):
            cols = slice(j * width, (j + 1) * width)
            part = dot(turned[0], z_ref[0, :, cols]) + dot(turned[1], z_ref[1, :, cols])
            blocks[4 * j : 4 * j + 4] = part.astype(BF16).reshape(4, deep, width)
        scatter_blocks(sem2, own_place(), blocks, keep, send)

    half = ((CUTS // 2, deep, width), BF16, "a")
    scratch = [
        pltpu.VMEM((2, slots, ff), BF16),
        pltpu.VMEM((2, slots, width), BF16),
        pltpu.VMEM((CUTS, deep, width), BF16),
        pltpu.SemaphoreType.DMA((4,)),
        pltpu.SemaphoreType.DMA((CUTS,)),
    ]
    ins = [(z, "a"), (dm, "a"), (recv, "a")]
    return run(body, ins, [half, half, ((8, width), F32, "v")], scratch, us=4)


def up_grads(lines, recv, weights, kept, dims):
    slots, width, ff = dims
    deep = width // 4
    shapes = all_sizes(dims)
    halves = (slice(0, slots), slice(slots, 2 * slots))
    names = ("gp", "h", "du", "dp", "dh", "small", "dm")
    given = ("gp", "h", "c", "du", "dp", "small")
    n_in = len(lines) + 3 + len(given)

    def body(*refs):
        vec = dict(zip(LINES, refs[: len(lines)]))
        recv_hbm, up_hbm, down_hbm = refs[len(lines) : len(lines) + 3]
        hbm = dict(zip(given, refs[len(lines) + 3 : n_in]))
        keep, send, sums, dp_hbm, small_hbm, dh_hbm = refs[n_in : n_in + 6]
        rest = refs[n_in + 6 :]
        w = {"up": rest[0], "down": rest[1]}
        r = dict(zip(names, rest[2 : 2 + len(names)]))
        c, d, blocks, sem, sem2 = rest[2 + len(names) :]
        moves = Moves(sem)
        lead = lax.axis_index("section") == 0
        for i, h in enumerate(halves):
            moves.start("c%d" % i, hbm["c"].at[i], c.at[h])
        moves.start("d0", hbm["du"].at[0], d.at[0])
        own = moves.make("d1", hbm["du"].at[1], d.at[1])

        @pl.when(jnp.logical_not(lead))
        def _():
            own.start()
            own.wait()

        @pl.when(lead)
        def _():
            inner = Moves(sem.at[pl.ds(4, 12)])
            inner.start("dm", recv_hbm, r["dm"])
            inner.start("down", down_hbm.at[0], w["down"])
            inner.start("gp", hbm["gp"].at[1], r["gp"])
            inner.start("up", up_hbm.at[0], w["up"])
            inner.start("h", hbm["h"].at[1], r["h"])
            inner.wait("dm")
            out = {"dp": dp_hbm.at[1]}

            def done(n):
                if n in out:
                    inner.start("save " + n, r[n], out[n])

            r["du"] = d.at[1]
            backward_mlp(r["dm"], vec, w, r, inner.wait, done)
            inner.start("save small", r["small"], small_hbm.at[1])
            inner.start("save dh", r["dh"], dh_hbm)
            inner.finish()

        for n in ("c0", "c1", "d0"):
            moves.wait(n)
        ones = jnp.ones((16, slots), BF16)
        turned = [c[h, :].T for h in halves]
        for j in range(4):
            cols = slice(j * width, (j + 1) * width)
            parts = [d[i, :, cols] for i in (0, 1)]
            sums[j] = (dot(ones, parts[0]) + dot(ones, parts[1]))[:8]
            part = (dot(turned[0], parts[0]) + dot(turned[1], parts[1])).astype(BF16)
            blocks[4 * j : 4 * j + 4] = part.reshape(4, deep, width)
        scatter_blocks(sem2, own_place(), blocks, keep, send)

    half = ((CUTS // 2, deep, width), BF16, "a")
    ins = [(v, "v") for v in lines] + [(recv, "a"), (weights[2], "a"), (weights[3], "a")]
    ins += [(kept[n], "a") for n in given]
    outs = [half, half, ((4, 8, width), F32, "v")]
    outs += [(kept[n].shape, kept[n].dtype, "a") for n in ("dp", "small")]
    outs += [((slots, width), F32, "a")]
    wshapes = weight_sizes(width, ff)
    scratch = [pltpu.VMEM(wshapes["up"], BF16), pltpu.VMEM(wshapes["down"], BF16)]
    scratch += [pltpu.VMEM(*shapes[n]) for n in names]
    scratch += [
        pltpu.VMEM((2 * slots, width), BF16),
        pltpu.VMEM((2, slots, ff), BF16),
        pltpu.VMEM((CUTS, deep, width), BF16),
        pltpu.SemaphoreType.DMA((16,)),
        pltpu.SemaphoreType.DMA((CUTS,)),
    ]
    return run(body, ins, outs, scratch, {n_in - 2: 3, n_in - 1: 4}, us=6)


def attention_grads(lines, tokens, weights, kept, dh, grads, down_sums, up_sums, dims):
    slots, width, ff = dims
    deep = width // 4
    tall = deep + 16
    shapes = all_sizes(dims)
    names = (
        "dp", "dh", "inv", "ot", "v", "e", "kt", "qt", "s", "ds", "g", "center", "dot", "dqkv",
        "small",
    )
    loads = ("inv", "v", "e", "kt", "qt")
    given = ("a", "ot", "dp", "dqkv", "small") + loads
    n_in = len(lines) + 7 + len(given)

    def body(*refs):
        vec = dict(zip(LINES, refs[: len(lines)]))
        tokens_hbm, out_hbm, qkv_hbm, dh_hbm, grads_in, down_ref, up_ref = refs[
            len(lines) : len(lines) + 7
        ]
        hbm = dict(zip(given, refs[len(lines) + 7 : n_in]))
        keep, send, grads_hbm = refs[n_in : n_in + 3]
        rest = refs[n_in + 3 :]
        w = {"out": rest[0], "qkv": rest[1]}
        r = dict(zip(names, rest[2 : 2 + len(names)]))
        x, a, d, o, p, s, blocks, sem, sem2 = rest[2 + len(names) :]
        moves = Moves(sem)
        lead = lax.axis_index("section") == 0
        moves.start("p1", hbm["dp"].at[1], p.at[1])
        moves.start("o1", hbm["ot"].at[1], o.at[1])
        moves.start("s1", hbm["small"].at[1], s.at[1])
        own = moves.make("d1", hbm["dqkv"].at[1], d.at[1])

        @pl.when(jnp.logical_not(lead))
        def _():
            own.start()

        @pl.when(lead)
        def _():
            inner = Moves(sem.at[pl.ds(12, 12)])
            inner.start("out", out_hbm.at[0], w["out"])
            for n in loads:
                inner.start(n, hbm[n].at[1], r[n])
            inner.start("qkv", qkv_hbm.at[0], w["qkv"])
            inner.start("x", tokens_hbm.at[1, 0], x)
            inner.start("dh", dh_hbm, r["dh"])
            for n in ("p1", "o1", "s1"):
                moves.made[n].wait()
            r.update(dp=p.at[1], ot=o.at[1], dqkv=d.at[1], small=s.at[1])

            def wait(n):
                if n == "qkv":
                    inner.wait("x")
                    inner.wait("dh")
                inner.wait(n)

            backward_attention(x, x, vec, w, r, wait, nothing)
            inner.start("g", x, grads_hbm.at[1])
            inner.finish()

        @pl.when(jnp.logical_not(lead))
        def _():
            for n in ("p1", "o1", "s1", "d1"):
                moves.made[n].wait()

        for n in ("p1", "o1", "s1", "d1"):
            moves.made.pop(n)
        moves.start("p0", hbm["dp"].at[0], p.at[0])
        moves.start("o0", hbm["ot"].at[0], o.at[0])
        moves.start("s0", hbm["small"].at[0], s.at[0])
        moves.start("d0", hbm["dqkv"].at[0], d.at[0])
        moves.start("a0", hbm["a"].at[0], a.at[0])
        moves.start("a1", hbm["a"].at[1], a.at[1])
        moves.finish()
        ones = jnp.ones((16, slots), BF16)
        turned = [a[i].T for i in (0, 1)]
        both = s[0] + s[1]
        rows = [
            both[A_GAIN_G : A_GAIN_G + 1], both[A_SHIFT_G : A_SHIFT_G + 1], None, None,
            (dot(ones, p[0]) + dot(ones, p[1]))[:1],
            both[M_GAIN_G : M_GAIN_G + 1], both[M_SHIFT_G : M_SHIFT_G + 1],
            down_ref[:1], up_ref[0, :1], up_ref[1, :1], up_ref[2, :1], up_ref[3, :1],
        ]
        for j in range(3):
            parts = [d[i, j].reshape(width, slots) for i in (0, 1)]
            if j != 1:
                rows[2 + j // 2] = (dot_nt(ones, parts[0]) + dot_nt(ones, parts[1]))[:1]
            part = (dot_nt(turned[0], parts[0]) + dot_nt(turned[1], parts[1])).astype(BF16)
            blocks[4 * j : 4 * j + 4, :deep] = part.reshape(4, deep, width)
        mixed = [o[i].reshape(width, slots).astype(BF16) for i in (0, 1)]
        part = dot(mixed[0], p[0]) + dot(mixed[1], p[1])
        blocks[12:16, :deep] = part.astype(BF16).reshape(4, deep, width)
        for i in range(CUTS):
            line = rows[i] if i < 12 else jnp.zeros((1, width), F32)
            blocks[i, deep:] = jnp.broadcast_to(line, (16, width)).astype(BF16)
        scatter_blocks(sem2, own_place(), blocks, keep, send)

    ins = [(v, "v") for v in lines] + [(tokens, "a"), (weights[1], "a"), (weights[0], "a")]
    ins += [(dh, "a"), (grads, "a"), (down_sums, "v"), (up_sums, "v")]
    ins += [(kept[n], "a") for n in given]
    half = ((CUTS // 2, tall, width), BF16, "a")
    outs = [half, half, (grads.shape, grads.dtype, "a")]
    wshapes = weight_sizes(width, ff)
    scratch = [pltpu.VMEM(wshapes["out"], BF16), pltpu.VMEM(wshapes["qkv"], BF16)]
    scratch += [pltpu.VMEM(*shapes[n]) for n in names]
    scratch += [pltpu.VMEM((slots, width), BF16)]
    scratch += [pltpu.VMEM((2, *shapes[n][0]), shapes[n][1]) for n in ("a", "dqkv", "ot", "dp", "small")]
    scratch += [
        pltpu.VMEM((CUTS, tall, width), BF16),
        pltpu.SemaphoreType.DMA((24,)),
        pltpu.SemaphoreType.DMA((CUTS,)),
    ]
    return run(body, ins, outs, scratch, {len(lines) + 4: 2}, us=12)


def block(own, other, p):
    place = jnp.bitwise_xor(p, own_place())
    mine = own[place // 2]
    theirs = other[place // 2]
    odd = jnp.bitwise_and(place, 1)
    return jnp.where(odd == 1, theirs, mine).astype(F32)


def down_out(own, other, dims):
    slots, width, ff = dims

    def body(own_ref, other_ref, out):
        for j in range(4):
            part = [block(own_ref, other_ref, 4 * j + i) for i in range(4)]
            out[0, j * width : (j + 1) * width, :] = jnp.concatenate(part, 0).T

    return run(body, [(own, "v"), (other, "v")], [((1, ff, width), F32, "v")], [], us=3)[0]


def up_out(own, other, dims):
    slots, width, ff = dims
    deep = width // 4

    def body(own_ref, other_ref, out):
        for p in range(CUTS):
            j, i = p // 4, p % 4
            out[0, i * deep : (i + 1) * deep, j * width : (j + 1) * width] = block(
                own_ref, other_ref, p
            )

    return run(body, [(own, "v"), (other, "v")], [((1, width, ff), F32, "v")], [], us=3)[0]


def attention_out(own, other, dims):
    slots, width, ff = dims
    deep = width // 4

    def body(own_ref, other_ref, qkv, out, *lines):
        for p in range(CUTS):
            j, i = p // 4, p % 4
            got = block(own_ref, other_ref, p)
            if j < 3:
                qkv[0, i * deep : (i + 1) * deep, j * width : (j + 1) * width] = got[:deep]
            else:
                out[0, i * deep : (i + 1) * deep, :] = got[:deep]
            if p < 8:
                lines[p][...] = got[deep : deep + 1]
            elif p < 12:
                lines[8][:, (p - 8) * width : (p - 7) * width] = got[deep : deep + 1]

    outs = [((1, width, 3 * width), F32, "v"), ((1, width, width), F32, "v")]
    outs += [((1, width), F32, "v")] * 8 + [((1, ff), F32, "v")]
    return run(body, [(own, "v"), (other, "v")], outs, [], us=3)


def swapped(x, bits):
    return lax.ppermute(x, "dp", [(i, i ^ bits) for i in range(CUTS)])


def added(*parts):
    total = parts[0].astype(F32)
    for x in parts[1:]:
        total = total + x.astype(F32)
    return total.astype(BF16)


def all_reduced(keep, send):
    if lax.axis_size("dp") != CUTS:
        return lax.psum(keep, "dp"), lax.psum(send, "dp")
    u = added(keep, swapped(send, 1))
    u = u.reshape(4, 2, *u.shape[1:])
    u = added(u[:, 0], swapped(u[:, 1], 2))
    u = added(u[0], *[swapped(u[j], 4 * j) for j in (1, 2, 3)])
    u = jnp.stack([u] + [swapped(u, 4 * j) for j in (1, 2, 3)])
    u = jnp.stack([u, swapped(u, 2)], 1)
    u = u.reshape(8, *u.shape[2:])
    return u, swapped(u, 1)


def shards(
    tokens, cotangent, views, attn_gain, attn_shift, qkv_weight, query_bias, value_bias,
    out_weight, out_bias, mlp_gain, mlp_shift, up_weight, up_bias, down_weight, down_bias,
):
    dims = (tokens.shape[2], tokens.shape[3], up_bias.shape[1])
    weights = (qkv_weight, out_weight, up_weight, down_weight)
    lines = (
        attn_gain, attn_shift, query_bias, value_bias, out_bias, mlp_gain, mlp_shift, down_bias,
        up_bias,
    )

    def advance(t, carry):
        recv, bufs = carry
        step = jnp.reshape(t, (1,))
        send, bufs = cell(step, views, lines, tokens, cotangent, recv, weights, bufs, dims)
        return lax.ppermute(send, "section", [(0, 1), (1, 0)]), bufs

    recv, bufs = lax.fori_loop(0, STEPS, advance, blank(dims))
    outs, grads = bufs[:2]
    kept = dict(zip(SAVED + TERMS, bufs[2:]))
    keep, send, down_sums = down_grads(kept["z"], kept["dm"], recv, dims)
    down_sum = all_reduced(keep, send)
    keep, send, up_sums, kept["dp"], kept["small"], dh = up_grads(lines, recv, weights, kept, dims)
    up_sum = all_reduced(keep, send)
    keep, send, grads = attention_grads(
        lines, tokens, weights, kept, dh, grads, down_sums, up_sums, dims
    )
    attention_sum = all_reduced(keep, send)
    g_down = down_out(*down_sum, dims)
    g_up = up_out(*up_sum, dims)
    g_qkv, g_out, *rows = attention_out(*attention_sum, dims)
    g_ag, g_as, g_qb, g_vb, g_ob, g_mg, g_ms, g_db, g_ub = rows
    return (
        outs[None, :, None], grads[None, :, None], g_ag, g_as, g_qkv, g_qb, g_vb, g_out, g_ob,
        g_mg, g_ms, g_up, g_ub, g_down, g_db,
    )


def solution(mesh):
    scene = P(None, "dp", None, None)
    line = P("section", None)
    table = P("section", None, None)
    kept = P("section", None, "dp", None, None)
    kinds = (line, line, table, line, line, table, line, line, line, table, line, table, line)
    return jax.shard_map(
        shards,
        mesh=mesh,
        in_specs=(scene, scene, P(None, "dp")) + kinds,
        out_specs=(kept, kept) + kinds,
        check_vma=False,
    )
```

```python
import jax
import jax.numpy as jnp
from jax import lax
from jax.experimental import pallas as pl
from jax.experimental.pallas import tpu as pltpu
from jax.sharding import PartitionSpec as P

HEADS = 6
HEAD = 64
PATCHES = 64
EPSILON = 1e-06
MASKED = -1e30
LANES = 128
CUTS = 16
F32 = jnp.float32
BF16 = jnp.bfloat16
VMEM_LIMIT = 16 * 2**20
BIG = 55 * 2**20


def dot(a, b):
    return lax.dot_general(a, b, (((1,), (0,)), ((), ())), preferred_element_type=F32)


def dot_nt(a, b):
    return lax.dot_general(a, b, (((1,), (1,)), ((), ())), preferred_element_type=F32)


def unit_rows(values):
    center = values - jnp.mean(values, -1, keepdims=True)
    spread = jnp.mean(center * center, -1, keepdims=True)
    scale = lax.rsqrt(spread + EPSILON)
    return center * scale, scale


def row(vec, name):
    return vec[name][...].astype(F32)


LINES = ("ag", "as", "qb", "vb", "ob", "mg", "ms", "db", "ub")
CHUNK = 256


def padded(rows, odd):
    zero = jnp.zeros_like(rows)
    return jnp.concatenate([zero, rows] if odd else [rows, zero], 0)


def forward(x_ref, y_ref, count, vec, w, r, wait, done):
    slots, width = x_ref.shape
    ub = row(vec, "ub")
    ff = ub.shape[1]

    unit, _ = unit_rows(x_ref[...].astype(F32))
    a = (unit * row(vec, "ag") + row(vec, "as")).astype(BF16)
    r["a"][...] = a
    wait("qkv")
    q = dot(a, w["qkv"][:, :width]) + row(vec, "qb")
    r["qt"][...] = (q * HEAD**-0.5).astype(BF16).T.reshape(HEADS, HEAD, slots)
    k = dot(a, w["qkv"][:, width : 2 * width]).astype(BF16)
    r["kt"][...] = k.T.reshape(HEADS, HEAD, slots)
    v = (dot(a, w["qkv"][:, 2 * width :]) + row(vec, "vb")).astype(BF16)
    r["vt"][...] = v.T.reshape(HEADS, HEAD, slots)
    for p in range(HEADS // 2):
        r["k"][p] = k[:, p * 2 * HEAD : (p + 1) * 2 * HEAD]
        r["v"][p] = v[:, p * 2 * HEAD : (p + 1) * 2 * HEAD]
    for n in ("a", "qt", "k", "kt", "v"):
        done(n)
    groups = slots // PATCHES
    shift = [jnp.where(g < count, 0.0, MASKED).astype(F32) for g in range(groups)]

    last = HEADS - 1

    def scores(h, odd):
        r["s"][odd] = dot(r["k"][h // 2], padded(r["qt"][h], odd))

    def soften(h, odd):
        s_ref = r["s"].at[odd]
        for c in range(slots // LANES):
            cols = slice(c * LANES, (c + 1) * LANES)
            peak = s_ref[0:PATCHES, cols]
            for g in range(1, groups):
                block = s_ref[g * PATCHES : (g + 1) * PATCHES, cols]
                peak = jnp.maximum(peak, block if g < 2 else block + shift[g])
            peak = jnp.max(peak, 0, keepdims=True)
            acc = jnp.zeros((PATCHES, LANES), F32)
            for g in range(groups):
                block = s_ref[g * PATCHES : (g + 1) * PATCHES, cols]
                e = jnp.exp(block - (peak - shift[g]))
                acc = acc + e
                r["e"][h, g * PATCHES : (g + 1) * PATCHES, cols] = e.astype(BF16)
            r["inv"][h, :, cols] = 1.0 / jnp.sum(acc, 0, keepdims=True)

    def mix(h):
        r["ot"][h] = dot(r["vt"][h], r["e"][h]) * r["inv"][h]

    def pair(i):
        h = 2 * i
        scores(h + 1, 1)
        soften(h, 0)
        if h:
            mix(h - 1)
        if h + 2 < HEADS:
            scores(h + 2, 0)
        soften(h + 1, 1)
        mix(h)

    scores(0, 0)
    for i in range(HEADS // 2):
        pair(i)
    mix(last)
    for n in ("e", "inv", "ot"):
        done(n)
    wait("out")
    o = r["ot"][...].reshape(width, slots).astype(BF16).T
    hidden = x_ref[...].astype(F32) + dot(o, w["out"][...]) + row(vec, "ob")
    r["h"][...] = hidden
    done("h")
    unit, _ = unit_rows(hidden)
    c = (unit * row(vec, "mg") + row(vec, "ms")).astype(BF16)
    r["c"][...] = c
    done("c")
    wait("up")
    for f in range(0, ff, CHUNK):
        cols = slice(f, f + CHUNK)
        u = dot(c, w["up"][:, cols]) + ub[:, cols]
        phi = 0.5 + 0.5 * lax.erf(u * 0.5**0.5)
        density = jnp.exp(-0.5 * u * u) * 0.3989422804014327
        r["z"][:, cols] = (u * phi).astype(BF16)
        r["gp"][:, cols] = (phi + u * density).astype(BF16)
    done("z")
    done("gp")
    wait("down")
    y_ref[...] = (r["h"][...] + dot(r["z"][...], w["down"][...]) + row(vec, "db")).astype(BF16)


def nothing(name):
    pass


def sizes(slots, width, ff):
    turned = ((HEADS, HEAD, slots), BF16)
    pairs = ((HEADS // 2, slots, 2 * HEAD), BF16)
    return dict(
        a=((slots, width), BF16),
        qt=turned,
        k=pairs,
        kt=turned,
        v=pairs,
        vt=turned,
        s=((2, slots, slots), F32),
        e=((HEADS, slots, slots), BF16),
        inv=((HEADS, 1, slots), F32),
        ot=((HEADS, HEAD, slots), F32),
        h=((slots, width), F32),
        c=((slots, width), BF16),
        z=((slots, ff), BF16),
        gp=((slots, ff), BF16),
    )


def norm_back(grad, gain, unit, scale):
    t = grad * gain
    inner = jnp.mean(t, -1, keepdims=True)
    along = jnp.mean(t * unit, -1, keepdims=True)
    return scale * (t - inner - unit * along)


M_GAIN_G, M_SHIFT_G, A_GAIN_G, A_SHIFT_G = range(4)


def backward_mlp(grad_ref, vec, w, r, wait, done):
    slots, width = grad_ref.shape
    ff = r["du"].shape[1]
    wait("down")
    wait("gp")
    low = grad_ref[...]
    for f in range(0, ff, CHUNK):
        cols = slice(f, f + CHUNK)
        dz = dot_nt(low, w["down"][cols, :])
        r["du"][:, cols] = (dz * r["gp"][:, cols].astype(F32)).astype(BF16)
    done("du")
    wait("up")
    dc = dot_nt(r["du"][...], w["up"][...])
    wait("h")
    unit, scale = unit_rows(r["h"][...])
    r["small"][M_GAIN_G : M_GAIN_G + 1, :] = jnp.sum(dc * unit, 0, keepdims=True)
    r["small"][M_SHIFT_G : M_SHIFT_G + 1, :] = jnp.sum(dc, 0, keepdims=True)
    dh = low.astype(F32) + norm_back(dc, row(vec, "mg"), unit, scale)
    r["dh"][...] = dh
    r["dp"][...] = dh.astype(BF16)
    done("dp")


def backward_attention(x_ref, g_ref, vec, w, r, wait, done):
    slots, width = x_ref.shape
    wait("out")
    dot_t = dot_nt(w["out"][...], r["dp"][...])
    r["dot"][...] = dot_t.reshape(HEADS, HEAD, slots)

    last = HEADS - 1
    for n in ("inv", "ot", "v", "e", "kt", "qt"):
        wait(n)

    def spread(h, odd):
        g = (r["dot"][h] * r["inv"][h]).astype(BF16)
        r["g"][odd] = g
        r["center"][odd] = jnp.sum(g.astype(F32) * r["ot"][h], 0, keepdims=True)
        r["s"][odd] = dot(r["v"][h // 2], padded(g, odd))

    def weigh(h, odd):
        s_ref = r["s"].at[odd]
        for c in range(slots // LANES):
            cols = slice(c * LANES, (c + 1) * LANES)
            center = r["center"][odd, :, cols]
            for b in range(0, slots, PATCHES):
                block = s_ref[b : b + PATCHES, cols] - center
                r["ds"][odd, b : b + PATCHES, cols] = (
                    block * r["e"][h, b : b + PATCHES, cols].astype(F32)
                ).astype(BF16)

    def gather(h, odd):
        ds = r["ds"][odd]
        r["dqkv"][0, h] = (dot(r["kt"][h], ds) * HEAD**-0.5).astype(BF16)
        r["dqkv"][1, h] = dot_nt(r["qt"][h], ds).astype(BF16)

    def gather_v(h, odd):
        r["dqkv"][2, h] = dot_nt(r["g"][odd], r["e"][h]).astype(BF16)

    def pair(i):
        h = 2 * i
        gather_v(h, 0)
        spread(h + 1, 1)
        weigh(h, 0)
        if h:
            gather(h - 1, 1)
        gather_v(h + 1, 1)
        if h + 2 < HEADS:
            spread(h + 2, 0)
        weigh(h + 1, 1)
        gather(h, 0)

    spread(0, 0)
    for i in range(HEADS // 2):
        pair(i)
    gather(last, 1)
    done("dqkv")

    wait("qkv")
    da = dot(w["qkv"][...], r["dqkv"][...].reshape(3 * width, slots)).T
    unit, scale = unit_rows(x_ref[...].astype(F32))
    r["small"][A_GAIN_G : A_GAIN_G + 1, :] = jnp.sum(da * unit, 0, keepdims=True)
    r["small"][A_SHIFT_G : A_SHIFT_G + 1, :] = jnp.sum(da, 0, keepdims=True)
    done("small")
    g_ref[...] = (r["dh"][...] + norm_back(da, row(vec, "ag"), unit, scale)).astype(BF16)


def back_sizes(slots, width, ff):
    return dict(
        du=((slots, ff), BF16),
        dh=((slots, width), F32),
        dp=((slots, width), BF16),
        dot=((HEADS, HEAD, slots), F32),
        ds=((2, slots, slots), BF16),
        g=((2, HEAD, slots), BF16),
        center=((2, 1, slots), F32),
        dqkv=((3, HEADS, HEAD, slots), BF16),
        small=((8, width), F32),
    )


WEIGHTS = ("qkv", "out", "up", "down")
SAVED = ("a", "qt", "kt", "v", "e", "inv", "ot", "h", "c", "z", "gp")
TERMS = ("du", "dp", "dqkv", "small", "dm")
STEPS = 3


def run(body, ins, outs, scratch, aliases=None, us=1, limit=VMEM_LIMIT):
    space = {"s": pltpu.SMEM, "v": pltpu.VMEM, "a": pl.ANY}
    return pl.pallas_call(
        body,
        out_shape=[jax.ShapeDtypeStruct(s, t) for s, t, _ in outs],
        in_specs=[pl.BlockSpec(memory_space=space[k]) for _, k in ins],
        out_specs=[pl.BlockSpec(memory_space=space[k]) for _, _, k in outs],
        scratch_shapes=scratch,
        input_output_aliases=aliases or {},
        compiler_params=pltpu.CompilerParams(vmem_limit_bytes=limit),
        cost_estimate=pl.CostEstimate(
            flops=us * 10**9, bytes_accessed=us * 2 * 10**6, transcendentals=0
        ),
    )(*[x for x, _ in ins])


def weight_sizes(width, ff):
    return dict(qkv=(width, 3 * width), out=(width, width), up=(width, ff), down=(ff, width))


def all_sizes(dims):
    slots, width, ff = dims
    return {**sizes(*dims), **back_sizes(*dims), "dm": ((slots, width), BF16)}


class Moves:
    def __init__(self, sem, used=0):
        self.sem = sem
        self.used = used
        self.made = {}

    def make(self, name, src, dst):
        self.made[name] = pltpu.make_async_copy(src, dst, self.sem.at[self.used])
        self.used += 1
        return self.made[name]

    def start(self, name, src, dst):
        self.make(name, src, dst).start()

    def wait(self, name):
        if name in self.made:
            self.made.pop(name).wait()

    def finish(self):
        for name in list(self.made):
            self.wait(name)


def blank(dims):
    slots, width, _ = dims
    shapes = all_sizes(dims)
    outs = [((slots, width), BF16, "a")] + [((2, slots, width), BF16, "a")] * 2
    outs += [((2, *shapes[n][0]), shapes[n][1], "a") for n in SAVED + TERMS]

    def body(*refs):
        pass

    got = run(body, [], outs, [])
    return got[0], tuple(got[1:])


def cell(step, views, lines, tokens, cotangent, recv, weights, bufs, dims):
    slots, width, ff = dims
    shapes = all_sizes(dims)
    wshapes = weight_sizes(width, ff)
    names = [n for n in shapes if n != "dm"]
    n_in = 2 + len(lines) + 3 + 4
    loads = ("gp", "h", "inv", "ot", "v", "e", "kt", "qt")

    def body(*refs):
        step_ref, views_ref = refs[:2]
        vec = dict(zip(LINES, refs[2 : 2 + len(lines)]))
        tokens_hbm, cot_hbm, recv_hbm = refs[2 + len(lines) : 5 + len(lines)]
        w_hbm = dict(zip(WEIGHTS, refs[5 + len(lines) : n_in]))
        rest = refs[n_in + len(bufs) :]
        send_hbm, outs_hbm, grads_hbm = rest[:3]
        kept = dict(zip(SAVED + TERMS, rest[3:]))
        rest = rest[3 + len(SAVED + TERMS) :]
        w = dict(zip(WEIGHTS, rest[:4]))
        r = dict(zip(names, rest[4 : 4 + len(names)]))
        x, dm, y, sem = rest[4 + len(names) :]
        moves = Moves(sem)
        t = step_ref[0]
        lead = lax.axis_index("section") == 0
        run_f = jnp.where(lead, t < 2, t > 0)
        run_b = jnp.where(lead, t == 2, t > 0)
        slot = jnp.where(lead, t % 2, jnp.maximum(t - 1, 0))
        only_b = jnp.logical_and(lead, run_b)
        not_lead = jnp.logical_not(lead)
        token_copy = moves.make("x", tokens_hbm.at[slot, 0], x)
        recv_copy = pltpu.make_async_copy(recv_hbm, x, token_copy_sem(moves, "x"))
        cot_copy = moves.make("dm", cot_hbm.at[slot, 0], dm)
        grad_copy = pltpu.make_async_copy(recv_hbm, dm, token_copy_sem(moves, "dm"))
        w_copy = {n: moves.make("w " + n, w_hbm[n].at[0], w[n]) for n in WEIGHTS}
        l_copy = {n: moves.make("l " + n, kept[n].at[slot], r[n]) for n in loads}
        s_copy = {n: moves.make("s " + n, r[n], kept[n].at[slot]) for n in SAVED}
        b_copy = {n: moves.make("b " + n, r[n], kept[n].at[slot]) for n in TERMS[:4]}
        b_copy["dm"] = moves.make("b dm", dm, kept["dm"].at[slot])
        y_copy = moves.make("y", y, outs_hbm.at[slot])
        g_copy = moves.make("g", x, grads_hbm.at[slot])
        y_send = moves.make("ys", y, send_hbm)
        g_send = moves.make("gs", x, send_hbm)

        @pl.when(run_f)
        def _():
            @pl.when(lead)
            def _():
                token_copy.start()

            @pl.when(not_lead)
            def _():
                recv_copy.start()

            for n in WEIGHTS:
                w_copy[n].start()

            @pl.when(not_lead)
            def _():
                cot_copy.start()

            token_copy.wait()
            forward(
                x, y, views_ref[slot, 0], vec, w, r,
                lambda n: w_copy[n].wait(), lambda n: s_copy[n].start() if n in s_copy else None,
            )
            y_copy.start()

            @pl.when(lead)
            def _():
                y_send.start()

            @pl.when(not_lead)
            def _():
                cot_copy.wait()

        @pl.when(only_b)
        def _():
            grad_copy.start()
            for n in ("down", "gp", "up", "h", "out", "inv", "ot", "v", "e", "kt", "qt", "qkv"):
                (w_copy if n in w_copy else l_copy)[n].start()
            token_copy.start()
            grad_copy.wait()
            for n in ("down", "gp", "up", "h"):
                (w_copy if n in w_copy else l_copy)[n].wait()

        @pl.when(run_b)
        def _():
            b_copy["dm"].start()
            backward_mlp(dm, vec, w, r, nothing, lambda n: b_copy[n].start())

            @pl.when(only_b)
            def _():
                for n in ("out", "inv", "ot", "v", "e", "kt", "qt", "qkv"):
                    (w_copy if n in w_copy else l_copy)[n].wait()
                token_copy.wait()

            backward_attention(x, x, vec, w, r, nothing, lambda n: b_copy[n].start())
            g_copy.start()

            @pl.when(not_lead)
            def _():
                g_send.start()

        @pl.when(run_f)
        def _():
            for n in SAVED:
                s_copy[n].wait()
            y_copy.wait()

            @pl.when(lead)
            def _():
                y_send.wait()

        @pl.when(run_b)
        def _():
            for n in TERMS:
                b_copy[n].wait()
            g_copy.wait()

            @pl.when(not_lead)
            def _():
                g_send.wait()

    ins = [(step, "s"), (views, "s")] + [(v, "v") for v in lines]
    ins += [(x, "a") for x in (tokens, cotangent, recv, *weights, *bufs)]
    outs = [((slots, width), BF16, "a")] + [(b.shape, b.dtype, "a") for b in bufs]
    scratch = [pltpu.VMEM(wshapes[n], BF16) for n in WEIGHTS]
    scratch += [pltpu.VMEM(*shapes[n]) for n in names]
    scratch += [pltpu.VMEM((slots, width), BF16)] * 3 + [pltpu.SemaphoreType.DMA((40,))]
    got = run(body, ins, outs, scratch, {n_in + i: 1 + i for i in range(len(bufs))}, us=15, limit=BIG)
    return got[0], tuple(got[1:])


def token_copy_sem(moves, name):
    return moves.sem.at[list(moves.made).index(name)]


class Scatter:
    def __init__(self, sem, blocks, keep_hbm, send_hbm):
        self.sem = sem
        self.blocks = blocks
        self.hbm = (keep_hbm, send_hbm)

    def start(self, p, rows, base=0):
        place = jnp.bitwise_xor(p, own_place())
        sem = self.sem.at[base + p]
        src = self.blocks.at[p, rows]
        for side in (0, 1):

            @pl.when(jnp.bitwise_and(place, 1) == side)
            def _():
                pltpu.make_async_copy(src, self.hbm[side].at[place // 2, rows], sem).start()

    def finish(self, rows, base=0):
        for p in range(CUTS):
            src = self.blocks.at[p, rows]
            pltpu.make_async_copy(src, self.hbm[0].at[0, rows], self.sem.at[base + p]).wait()


def with_ones(rows):
    return jnp.concatenate([rows, jnp.ones((16, rows.shape[1]), BF16)], 0)


def own_place():
    return lax.axis_index("dp") if lax.axis_size("dp") == CUTS else 0


def mlp_grads(lines, recv, weights, kept, dims):
    slots, width, ff = dims
    deep = width // 4
    shapes = all_sizes(dims)
    names = ("gp", "h", "du", "dp", "dh", "small")
    given = ("gp", "h", "c", "z", "dm", "du", "dp", "small")
    n_in = len(lines) + 3 + len(given)

    def body(*refs):
        vec = dict(zip(LINES, refs[: len(lines)]))
        recv_hbm, up_hbm, down_hbm = refs[len(lines) : len(lines) + 3]
        hbm = dict(zip(given, refs[len(lines) + 3 : n_in]))
        keep, send, sums, dp_hbm, small_hbm, dh_hbm = refs[n_in : n_in + 6]
        rest = refs[n_in + 6 :]
        w = {"up": rest[0], "down": rest[1]}
        r = dict(zip(names, rest[2 : 2 + len(names)]))
        m, z, c, d, turned_ref, blocks, sem, sem2 = rest[2 + len(names) :]
        moves = Moves(sem)
        inner = Moves(sem, 16)
        lead = lax.axis_index("section") == 0
        other = jnp.logical_not(lead)
        half = [slice(0, slots), slice(slots, 2 * slots)]
        m1 = moves.make("m1", hbm["dm"].at[1], m.at[half[1]])
        m1_recv = pltpu.make_async_copy(recv_hbm, m.at[half[1]], sem.at[0])
        d1 = moves.make("d1", hbm["du"].at[1], d.at[half[1]])
        moves.made.pop("d1")
        early = [
            inner.make("down", down_hbm.at[0], w["down"]),
            inner.make("gp", hbm["gp"].at[1], r["gp"]),
            inner.make("up", up_hbm.at[0], w["up"]),
            inner.make("h", hbm["h"].at[1], r["h"]),
        ]
        late = {
            "dp": inner.make("save dp", r["dp"], dp_hbm.at[1]),
            "small": inner.make("save small", r["small"], small_hbm.at[1]),
            "dh": inner.make("save dh", r["dh"], dh_hbm),
        }

        @pl.when(lead)
        def _():
            m1_recv.start()

        @pl.when(other)
        def _():
            m1.start()

        moves.start("m0", hbm["dm"].at[0], m.at[half[0]])
        for i in (0, 1):
            moves.start("z%d" % i, hbm["z"].at[i], z.at[half[i]])

        @pl.when(other)
        def _():
            d1.start()

        @pl.when(lead)
        def _():
            for copy in early:
                copy.start()

        for i in (0, 1):
            moves.start("c%d" % i, hbm["c"].at[i], c.at[half[i]])
        moves.start("d0", hbm["du"].at[0], d.at[half[0]])
        scatter = Scatter(sem2, blocks, keep, send)
        upper, lower = slice(0, deep), slice(deep, 2 * deep)
        moves.wait("m1")
        moves.wait("m0")
        turned = m[...].T
        sums[4] = dot(jnp.ones((16, 2 * slots), BF16), m[...])[:8]
        turned_ref[:width] = turned
        moves.wait("z0")
        moves.wait("z1")

        def down_part(j, carry):
            cols = pl.ds(pl.multiple_of(j * width, width), width)
            part = dot(turned_ref[:width], z[:, cols]).astype(BF16)
            blocks[pl.ds(4 * j, 4), upper] = part.reshape(4, deep, width)
            for i in range(4):
                scatter.start(4 * j + i, upper)
            return carry

        lax.fori_loop(0, 4, down_part, 0)

        @pl.when(other)
        def _():
            d1.wait()

        @pl.when(lead)
        def _():
            def done(n):
                if n == "dp":
                    late[n].start()

            r["du"] = d.at[half[1]]
            backward_mlp(m.at[half[1]], vec, w, r, inner.wait, done)
            late["small"].start()
            late["dh"].start()

        moves.finish()
        turned_ref[...] = with_ones(c[...].T)

        def up_part(j, carry):
            cols = pl.ds(pl.multiple_of(j * width, width), width)
            part = dot(turned_ref[...], d[:, cols])
            sums[j] = part[width : width + 8]
            blocks[pl.ds(4 * j, 4), lower] = part[:width].astype(BF16).reshape(4, deep, width)
            for i in range(4):
                scatter.start(4 * j + i, lower, CUTS)
            return carry

        lax.fori_loop(0, 4, up_part, 0)
        scatter.finish(upper)
        scatter.finish(lower, CUTS)

        @pl.when(lead)
        def _():
            for copy in late.values():
                copy.wait()

    half = ((CUTS // 2, 2 * deep, width), BF16, "a")
    ins = [(v, "v") for v in lines] + [(recv, "a"), (weights[2], "a"), (weights[3], "a")]
    ins += [(kept[n], "a") for n in given]
    outs = [half, half, ((5, 8, width), F32, "v")]
    outs += [(kept[n].shape, kept[n].dtype, "a") for n in ("dp", "small")]
    outs += [((slots, width), F32, "a")]
    wshapes = weight_sizes(width, ff)
    scratch = [pltpu.VMEM(wshapes["up"], BF16), pltpu.VMEM(wshapes["down"], BF16)]
    scratch += [pltpu.VMEM(*shapes[n]) for n in names]
    scratch += [
        pltpu.VMEM((2 * slots, width), BF16),
        pltpu.VMEM((2 * slots, ff), BF16),
        pltpu.VMEM((2 * slots, width), BF16),
        pltpu.VMEM((2 * slots, ff), BF16),
        pltpu.VMEM((width + 16, 2 * slots), BF16),
        pltpu.VMEM((CUTS, 2 * deep, width), BF16),
        pltpu.SemaphoreType.DMA((24,)),
        pltpu.SemaphoreType.DMA((2 * CUTS,)),
    ]
    return run(body, ins, outs, scratch, {n_in - 2: 3, n_in - 1: 4}, us=12, limit=BIG)


def attention_grads(lines, tokens, weights, kept, dh, grads, sums, dims):
    slots, width, ff = dims
    deep = width // 4
    tall = deep + 16
    shapes = all_sizes(dims)
    names = (
        "dp", "dh", "inv", "ot", "v", "e", "kt", "qt", "s", "ds", "g", "center", "dot", "dqkv",
        "small",
    )
    loads = ("inv", "v", "e", "kt", "qt")
    given = ("a", "ot", "dp", "dqkv", "small") + loads
    n_in = len(lines) + 6 + len(given)

    def body(*refs):
        vec = dict(zip(LINES, refs[: len(lines)]))
        tokens_hbm, out_hbm, qkv_hbm, dh_hbm, grads_in, sums_ref = refs[
            len(lines) : len(lines) + 6
        ]
        hbm = dict(zip(given, refs[len(lines) + 6 : n_in]))
        keep, send, grads_hbm = refs[n_in : n_in + 3]
        rest = refs[n_in + 3 :]
        w = {"out": rest[0], "qkv": rest[1]}
        r = dict(zip(names, rest[2 : 2 + len(names)]))
        x, a, d, o, p, s, turned_ref, lines_ref, blocks, sem, sem2 = rest[2 + len(names) :]
        moves = Moves(sem)
        inner = Moves(sem, 12)
        lead = lax.axis_index("section") == 0
        other = jnp.logical_not(lead)
        half = [slice(0, slots), slice(slots, 2 * slots)]
        place = {
            "dp": lambda i: p.at[half[i]],
            "a": lambda i: a.at[half[i]],
            "ot": lambda i: o.at[:, :, half[i]],
            "dqkv": lambda i: d.at[:, :, :, half[i]],
            "small": lambda i: s.at[i],
        }
        for n in ("dp", "ot", "small"):
            moves.start(n + "1", hbm[n].at[1], place[n](1))
        own = moves.make("dqkv1", hbm["dqkv"].at[1], place["dqkv"](1))
        early = [inner.make("out", out_hbm.at[0], w["out"])]
        early += [inner.make(n, hbm[n].at[1], r[n]) for n in loads]
        early += [
            inner.make("qkv", qkv_hbm.at[0], w["qkv"]),
            inner.make("x", tokens_hbm.at[1, 0], x),
            inner.make("dh", dh_hbm, r["dh"]),
        ]
        g_copy = inner.make("g", x, grads_hbm.at[1])

        @pl.when(other)
        def _():
            own.start()

        @pl.when(lead)
        def _():
            for copy in early:
                copy.start()

        for n in ("a", "dqkv", "ot", "dp", "small"):
            moves.start(n + "0", hbm[n].at[0], place[n](0))
        moves.start("a1", hbm["a"].at[1], place["a"](1))
        for n in ("dp1", "ot1", "small1"):
            moves.wait(n)

        @pl.when(lead)
        def _():
            r.update({n: place[n](1) for n in ("dp", "ot", "dqkv", "small")})

            def wait(n):
                if n == "qkv":
                    inner.wait("x")
                    inner.wait("dh")
                inner.wait(n)

            backward_attention(x, x, vec, w, r, wait, nothing)
            g_copy.start()

        @pl.when(other)
        def _():
            own.wait()

        moves.made.pop("dqkv1")
        moves.finish()
        scatter = Scatter(sem2, blocks, keep, send)
        full, deep_rows = slice(0, tall), slice(0, deep)
        turned_ref[...] = with_ones(a[...].T)

        def qkv_part(j, carry):
            part = dot_nt(turned_ref[...], d[j].reshape(width, 2 * slots))
            lines_ref[j] = part[width : width + 8]
            part = part[:width].astype(BF16).reshape(4, deep, width)
            blocks[pl.ds(4 * j, 4), deep_rows] = part
            return carry

        lax.fori_loop(0, 3, qkv_part, 0)
        part = dot(with_ones(o[...].reshape(width, 2 * slots).astype(BF16)), p[...])
        blocks[12:16, deep_rows] = part[:width].astype(BF16).reshape(4, deep, width)
        both = s[0] + s[1]
        rows = [
            both[A_GAIN_G : A_GAIN_G + 1], both[A_SHIFT_G : A_SHIFT_G + 1],
            lines_ref[0, :1], lines_ref[2, :1],
            part[width : width + 1],
            both[M_GAIN_G : M_GAIN_G + 1], both[M_SHIFT_G : M_SHIFT_G + 1],
            *[sums_ref[i, :1] for i in (4, 0, 1, 2, 3)],
        ]
        for i in range(CUTS):
            line = rows[i] if i < 12 else jnp.zeros((1, width), F32)
            blocks[i, deep:] = jnp.broadcast_to(line, (16, width)).astype(BF16)
            scatter.start(i, full)
        scatter.finish(full)

        @pl.when(lead)
        def _():
            g_copy.wait()

    ins = [(v, "v") for v in lines] + [(tokens, "a"), (weights[1], "a"), (weights[0], "a")]
    ins += [(dh, "a"), (grads, "a"), (sums, "v")]
    ins += [(kept[n], "a") for n in given]
    half = ((CUTS // 2, tall, width), BF16, "a")
    outs = [half, half, (grads.shape, grads.dtype, "a")]
    wshapes = weight_sizes(width, ff)
    scratch = [pltpu.VMEM(wshapes["out"], BF16), pltpu.VMEM(wshapes["qkv"], BF16)]
    scratch += [pltpu.VMEM(*shapes[n]) for n in names]
    scratch += [
        pltpu.VMEM((slots, width), BF16),
        pltpu.VMEM((2 * slots, width), BF16),
        pltpu.VMEM((3, HEADS, HEAD, 2 * slots), BF16),
        pltpu.VMEM((HEADS, HEAD, 2 * slots), F32),
        pltpu.VMEM((2 * slots, width), BF16),
        pltpu.VMEM((2, 8, width), F32),
        pltpu.VMEM((width + 16, 2 * slots), BF16),
        pltpu.VMEM((3, 8, width), F32),
    ]
    scratch += [
        pltpu.VMEM((CUTS, tall, width), BF16),
        pltpu.SemaphoreType.DMA((24,)),
        pltpu.SemaphoreType.DMA((CUTS,)),
    ]
    return run(body, ins, outs, scratch, {len(lines) + 4: 2}, us=12, limit=BIG)


def block(own, other, p):
    place = jnp.bitwise_xor(p, own_place())
    mine = own[place // 2]
    theirs = other[place // 2]
    odd = jnp.bitwise_and(place, 1)
    return jnp.where(odd == 1, theirs, mine).astype(F32)


def mlp_out(own, other, dims):
    slots, width, ff = dims
    deep = width // 4

    def body(own_ref, other_ref, down, up):
        for j in range(4):
            part = [block(own_ref, other_ref, 4 * j + i) for i in range(4)]
            down[0, j * width : (j + 1) * width, :] = jnp.concatenate(
                [v[:deep] for v in part], 0
            ).T
            up[0, :, j * width : (j + 1) * width] = jnp.concatenate([v[deep:] for v in part], 0)

    outs = [((1, ff, width), F32, "v"), ((1, width, ff), F32, "v")]
    return run(body, [(own, "v"), (other, "v")], outs, [], us=4)


def attention_out(own, other, dims):
    slots, width, ff = dims
    deep = width // 4

    def body(own_ref, other_ref, qkv, out, *lines):
        for p in range(CUTS):
            j, i = p // 4, p % 4
            got = block(own_ref, other_ref, p)
            if j < 3:
                qkv[0, i * deep : (i + 1) * deep, j * width : (j + 1) * width] = got[:deep]
            else:
                out[0, i * deep : (i + 1) * deep, :] = got[:deep]
            if p < 8:
                lines[p][...] = got[deep : deep + 1]
            elif p < 12:
                lines[8][:, (p - 8) * width : (p - 7) * width] = got[deep : deep + 1]

    outs = [((1, width, 3 * width), F32, "v"), ((1, width, width), F32, "v")]
    outs += [((1, width), F32, "v")] * 8 + [((1, ff), F32, "v")]
    return run(body, [(own, "v"), (other, "v")], outs, [], us=3)


def swapped(x, bits):
    return lax.ppermute(x, "dp", [(i, i ^ bits) for i in range(CUTS)])


def added(*parts):
    total = parts[0].astype(F32)
    for x in parts[1:]:
        total = total + x.astype(F32)
    return total.astype(BF16)


def tied(token, *xs):
    return lax.optimization_barrier((token, *xs))[1:]


def square_send(u):
    return [swapped(u[:, j], 2 * j) for j in (1, 2, 3)]


def square_gather(u):
    return [swapped(u, 2 * j) for j in (1, 2, 3)]


def shards(
    tokens, cotangent, views, attn_gain, attn_shift, qkv_weight, query_bias, value_bias,
    out_weight, out_bias, mlp_gain, mlp_shift, up_weight, up_bias, down_weight, down_bias,
):
    dims = (tokens.shape[2], tokens.shape[3], up_bias.shape[1])
    weights = (qkv_weight, out_weight, up_weight, down_weight)
    lines = (
        attn_gain, attn_shift, query_bias, value_bias, out_bias, mlp_gain, mlp_shift, down_bias,
        up_bias,
    )

    def advance(t, carry):
        recv, bufs = carry
        step = jnp.reshape(t, (1,))
        send, bufs = cell(step, views, lines, tokens, cotangent, recv, weights, bufs, dims)
        return lax.ppermute(send, "section", [(0, 1), (1, 0)]), bufs

    recv, bufs = lax.fori_loop(0, STEPS, advance, blank(dims))
    outs, grads = bufs[:2]
    kept = dict(zip(SAVED + TERMS, bufs[2:]))
    m_keep, m_send, sums, kept["dp"], kept["small"], dh = mlp_grads(
        lines, recv, weights, kept, dims
    )
    if lax.axis_size("dp") != CUTS:
        a_keep, a_send, grads = attention_grads(lines, tokens, weights, kept, dh, grads, sums, dims)
        m, m_other, a, a_other = lax.psum((m_keep, m_send, a_keep, a_send), "dp")
    else:
        m = added(m_keep, swapped(m_send, 1)).reshape(2, 4, *m_keep.shape[1:])
        m1 = square_send(m)
        (dh,) = tied(m, dh)
        a_keep, a_send, grads = attention_grads(lines, tokens, weights, kept, dh, grads, sums, dims)
        a_got = jnp.concatenate([swapped(v, 1) for v in jnp.split(a_send, 2)], 0)
        m1 = tied(a_keep, *m1)
        m = added(m[:, 0], *m1)
        m2 = swapped(m, 8)
        (a_got,) = tied(m, a_got)
        a = added(a_keep, a_got).reshape(2, 4, *a_keep.shape[1:])
        a1 = square_send(a)
        m2, *a1 = lax.optimization_barrier((m2, *a1))
        m = added(m, m2[::-1])
        m1 = square_gather(m)
        a = added(a[:, 0], *a1)
        a2 = swapped(a, 8)
        (a2,) = tied(m, a2)
        a = added(a, a2[::-1])
        a1 = square_gather(a)
        m1 = tied(a, *m1)
        m = jnp.stack([m, *m1], 1).reshape(8, *m.shape[1:])
        m_other = swapped(m, 1)
        a1 = tied(m, *a1)
        a = jnp.stack([a, *a1], 1).reshape(8, *a.shape[1:])
        a_other = swapped(a, 1)
    g_down, g_up = mlp_out(m, m_other, dims)
    g_qkv, g_out, *rows = attention_out(a, a_other, dims)
    g_ag, g_as, g_qb, g_vb, g_ob, g_mg, g_ms, g_db, g_ub = rows
    return (
        outs[None, :, None], grads[None, :, None], g_ag, g_as, g_qkv, g_qb, g_vb, g_out, g_ob,
        g_mg, g_ms, g_up, g_ub, g_down, g_db,
    )


def solution(mesh):
    scene = P(None, "dp", None, None)
    line = P("section", None)
    table = P("section", None, None)
    kept = P("section", None, "dp", None, None)
    kinds = (line, line, table, line, line, table, line, line, line, table, line, table, line)
    return jax.shard_map(
        shards,
        mesh=mesh,
        in_specs=(scene, scene, P(None, "dp")) + kinds,
        out_specs=(kept, kept) + kinds,
        check_vma=False,
    )
```

```python
import jax
import jax.numpy as jnp
from jax import lax
from jax.experimental import pallas as pl
from jax.experimental.pallas import tpu as pltpu
from jax.sharding import PartitionSpec as P

HEADS = 6
HEAD = 64
PATCHES = 64
EPSILON = 1e-06
MASKED = -1e30
LANES = 128
CUTS = 16
F32 = jnp.float32
BF16 = jnp.bfloat16
VMEM_LIMIT = 16 * 2**20
BIG = 52 * 2**20
MID = 52 * 2**20


def dot(a, b):
    return lax.dot_general(a, b, (((1,), (0,)), ((), ())), preferred_element_type=F32)


def dot_nt(a, b):
    return lax.dot_general(a, b, (((1,), (1,)), ((), ())), preferred_element_type=F32)


def unit_rows(values):
    center = values - jnp.mean(values, -1, keepdims=True)
    spread = jnp.mean(center * center, -1, keepdims=True)
    scale = lax.rsqrt(spread + EPSILON)
    return center * scale, scale


def row(vec, name):
    return vec[name][...].astype(F32)


LINES = ("ag", "as", "qb", "vb", "ob", "mg", "ms", "db", "ub")
CHUNK = 256
WIDE = 256


def padded(rows, odd):
    zero = jnp.zeros_like(rows)
    return jnp.concatenate([zero, rows] if odd else [rows, zero], 0)


def forward(x_ref, y_ref, count, vec, w, r, wait, done):
    slots, width = x_ref.shape
    ub = row(vec, "ub")
    ff = ub.shape[1]

    unit, _ = unit_rows(x_ref[...].astype(F32))
    a = (unit * row(vec, "ag") + row(vec, "as")).astype(BF16)
    r["a"][...] = a
    wait("qkv")
    q = dot(a, w["qkv"][:, :width]) + row(vec, "qb")
    r["qt"][...] = (q * HEAD**-0.5).astype(BF16).T.reshape(HEADS, HEAD, slots)
    k = dot(a, w["qkv"][:, width : 2 * width]).astype(BF16)
    r["kt"][...] = k.T.reshape(HEADS, HEAD, slots)
    v = (dot(a, w["qkv"][:, 2 * width :]) + row(vec, "vb")).astype(BF16)
    r["vt"][...] = v.T.reshape(HEADS, HEAD, slots)
    for p in range(HEADS // 2):
        r["k"][p] = k[:, p * 2 * HEAD : (p + 1) * 2 * HEAD]
        r["v"][p] = v[:, p * 2 * HEAD : (p + 1) * 2 * HEAD]
    for n in ("a", "qt", "k", "kt", "v"):
        done(n)
    groups = slots // PATCHES
    shift = [jnp.where(g < count, 0.0, MASKED).astype(F32) for g in range(groups)]

    last = HEADS - 1

    def scores(h, odd):
        r["s"][odd] = dot(r["k"][h // 2], padded(r["qt"][h], odd))

    def soften(h, odd):
        s_ref = r["s"].at[odd]
        for c in range(slots // WIDE):
            cols = slice(c * WIDE, (c + 1) * WIDE)
            peak = None
            for g in range(groups):
                block = s_ref[g * PATCHES : (g + 1) * PATCHES, cols]
                top = jnp.max(block.reshape(PATCHES // 8, 8, WIDE), 0)
                top = top if g < 2 else top + shift[g]
                peak = top if g == 0 else jnp.maximum(peak, top)
            peak = jnp.max(peak, 0, keepdims=True)
            acc = jnp.zeros((8, WIDE), F32)
            for g in range(groups):
                block = s_ref[g * PATCHES : (g + 1) * PATCHES, cols]
                e = jnp.exp(block - (peak - shift[g]))
                acc = acc + jnp.sum(e.reshape(PATCHES // 8, 8, WIDE), 0)
                r["e"][h, g * PATCHES : (g + 1) * PATCHES, cols] = e.astype(BF16)
            r["inv"][h, :, cols] = 1.0 / jnp.sum(acc, 0, keepdims=True)

    def mix(h):
        r["ot"][h] = dot(r["vt"][h], r["e"][h]) * r["inv"][h]

    def pair(i):
        h = 2 * i
        scores(h + 1, 1)
        soften(h, 0)
        if h:
            mix(h - 1)
        if h + 2 < HEADS:
            scores(h + 2, 0)
        soften(h + 1, 1)
        mix(h)

    scores(0, 0)
    for i in range(HEADS // 2):
        pair(i)
    mix(last)
    for n in ("e", "inv", "ot"):
        done(n)
    wait("out")
    o = r["ot"][...].reshape(width, slots).astype(BF16).T
    hidden = x_ref[...].astype(F32) + dot(o, w["out"][...]) + row(vec, "ob")
    r["h"][...] = hidden
    done("h")
    unit, _ = unit_rows(hidden)
    c = (unit * row(vec, "mg") + row(vec, "ms")).astype(BF16)
    r["c"][...] = c
    done("c")
    wait("up")
    for f in range(0, ff, CHUNK):
        cols = slice(f, f + CHUNK)
        u = dot(c, w["up"][:, cols]) + ub[:, cols]
        phi = 0.5 + 0.5 * lax.erf(u * 0.5**0.5)
        density = jnp.exp(-0.5 * u * u) * 0.3989422804014327
        r["z"][:, cols] = (u * phi).astype(BF16)
        r["gp"][:, cols] = (phi + u * density).astype(BF16)
    done("z")
    done("gp")
    wait("down")
    y_ref[...] = (r["h"][...] + dot(r["z"][...], w["down"][...]) + row(vec, "db")).astype(BF16)


def nothing(name):
    pass


def sizes(slots, width, ff):
    turned = ((HEADS, HEAD, slots), BF16)
    pairs = ((HEADS // 2, slots, 2 * HEAD), BF16)
    return dict(
        a=((slots, width), BF16),
        qt=turned,
        k=pairs,
        kt=turned,
        v=pairs,
        vt=turned,
        s=((2, slots, slots), F32),
        e=((HEADS, slots, slots), BF16),
        inv=((HEADS, 1, slots), F32),
        ot=((HEADS, HEAD, slots), F32),
        h=((slots, width), F32),
        c=((slots, width), BF16),
        z=((slots, ff), BF16),
        gp=((slots, ff), BF16),
    )


def norm_back(grad, gain, unit, scale):
    t = grad * gain
    inner = jnp.mean(t, -1, keepdims=True)
    along = jnp.mean(t * unit, -1, keepdims=True)
    return scale * (t - inner - unit * along)


M_GAIN_G, M_SHIFT_G, A_GAIN_G, A_SHIFT_G = range(4)


def backward_mlp(grad_ref, vec, w, r, wait, done):
    slots, width = grad_ref.shape
    ff = r["du"].shape[1]
    wait("down")
    wait("gp")
    low = grad_ref[...]
    for f in range(0, ff, CHUNK):
        cols = slice(f, f + CHUNK)
        dz = dot_nt(low, w["down"][cols, :])
        r["du"][:, cols] = (dz * r["gp"][:, cols].astype(F32)).astype(BF16)
    done("du")
    wait("up")
    dc = dot_nt(r["du"][...], w["up"][...])
    wait("h")
    unit, scale = unit_rows(r["h"][...])
    r["small"][M_GAIN_G : M_GAIN_G + 1, :] = jnp.sum(dc * unit, 0, keepdims=True)
    r["small"][M_SHIFT_G : M_SHIFT_G + 1, :] = jnp.sum(dc, 0, keepdims=True)
    dh = low.astype(F32) + norm_back(dc, row(vec, "mg"), unit, scale)
    r["dh"][...] = dh
    r["dp"][...] = dh.astype(BF16)
    done("dp")


def backward_attention(x_ref, g_ref, vec, w, r, wait, done):
    slots, width = x_ref.shape
    wait("out")
    dot_t = dot_nt(w["out"][...], r["dp"][...])
    r["dot"][...] = dot_t.reshape(HEADS, HEAD, slots)

    last = HEADS - 1
    for n in ("inv", "ot", "v", "e", "kt", "qt"):
        wait(n)

    def spread(h, odd):
        g = (r["dot"][h] * r["inv"][h]).astype(BF16)
        r["g"][odd] = g
        r["center"][odd] = jnp.sum(g.astype(F32) * r["ot"][h], 0, keepdims=True)
        r["s"][odd] = dot(r["v"][h // 2], padded(g, odd))

    def weigh(h, odd):
        s_ref = r["s"].at[odd]
        for c in range(slots // WIDE):
            cols = slice(c * WIDE, (c + 1) * WIDE)
            center = r["center"][odd, :, cols]
            for b in range(0, slots, PATCHES):
                block = s_ref[b : b + PATCHES, cols] - center
                r["ds"][odd, b : b + PATCHES, cols] = (
                    block * r["e"][h, b : b + PATCHES, cols].astype(F32)
                ).astype(BF16)

    def gather(h, odd):
        ds = r["ds"][odd]
        r["dqkv"][0, h] = (dot(r["kt"][h], ds) * HEAD**-0.5).astype(BF16)
        r["dqkv"][1, h] = dot_nt(r["qt"][h], ds).astype(BF16)

    def gather_v(h, odd):
        r["dqkv"][2, h] = dot_nt(r["g"][odd], r["e"][h]).astype(BF16)

    def pair(i):
        h = 2 * i
        gather_v(h, 0)
        spread(h + 1, 1)
        weigh(h, 0)
        if h:
            gather(h - 1, 1)
        gather_v(h + 1, 1)
        if h + 2 < HEADS:
            spread(h + 2, 0)
        weigh(h + 1, 1)
        gather(h, 0)

    spread(0, 0)
    for i in range(HEADS // 2):
        pair(i)
    gather(last, 1)
    done("dqkv")

    wait("qkv")
    da = dot(w["qkv"][...], r["dqkv"][...].reshape(3 * width, slots)).T
    unit, scale = unit_rows(x_ref[...].astype(F32))
    r["small"][A_GAIN_G : A_GAIN_G + 1, :] = jnp.sum(da * unit, 0, keepdims=True)
    r["small"][A_SHIFT_G : A_SHIFT_G + 1, :] = jnp.sum(da, 0, keepdims=True)
    done("small")
    g_ref[...] = (r["dh"][...] + norm_back(da, row(vec, "ag"), unit, scale)).astype(BF16)


def back_sizes(slots, width, ff):
    return dict(
        du=((slots, ff), BF16),
        dh=((slots, width), F32),
        dp=((slots, width), BF16),
        dot=((HEADS, HEAD, slots), F32),
        ds=((2, slots, slots), BF16),
        g=((2, HEAD, slots), BF16),
        center=((2, 1, slots), F32),
        dqkv=((3, HEADS, HEAD, slots), BF16),
        small=((8, width), F32),
    )


WEIGHTS = ("qkv", "out", "up", "down")
SAVED = ("a", "qt", "kt", "v", "e", "inv", "ot", "h", "c", "z", "gp")
TERMS = ("du", "dp", "dqkv", "small", "dm")
STEPS = 3


def run(body, ins, outs, scratch, aliases=None, us=1, limit=VMEM_LIMIT):
    space = {"s": pltpu.SMEM, "v": pltpu.VMEM, "a": pl.ANY}
    return pl.pallas_call(
        body,
        out_shape=[jax.ShapeDtypeStruct(s, t) for s, t, _ in outs],
        in_specs=[pl.BlockSpec(memory_space=space[k]) for _, k in ins],
        out_specs=[pl.BlockSpec(memory_space=space[k]) for _, _, k in outs],
        scratch_shapes=scratch,
        input_output_aliases=aliases or {},
        compiler_params=pltpu.CompilerParams(vmem_limit_bytes=limit),
        cost_estimate=pl.CostEstimate(
            flops=us * 10**9, bytes_accessed=us * 2 * 10**6, transcendentals=0
        ),
    )(*[x for x, _ in ins])


def weight_sizes(width, ff):
    return dict(qkv=(width, 3 * width), out=(width, width), up=(width, ff), down=(ff, width))


def all_sizes(dims):
    slots, width, ff = dims
    return {**sizes(*dims), **back_sizes(*dims), "dm": ((slots, width), BF16)}


class Moves:
    def __init__(self, sem, used=0):
        self.sem = sem
        self.used = used
        self.made = {}

    def make(self, name, src, dst):
        self.made[name] = pltpu.make_async_copy(src, dst, self.sem.at[self.used])
        self.used += 1
        return self.made[name]

    def start(self, name, src, dst):
        self.make(name, src, dst).start()

    def wait(self, name):
        if name in self.made:
            self.made.pop(name).wait()

    def finish(self):
        for name in list(self.made):
            self.wait(name)


def blank(dims):
    slots, width, _ = dims
    shapes = all_sizes(dims)
    outs = [((slots, width), BF16, "a")] + [((2, slots, width), BF16, "a")] * 2
    outs += [((2, *shapes[n][0]), shapes[n][1], "a") for n in SAVED + TERMS]

    def body(*refs):
        pass

    got = run(body, [], outs, [])
    return got[0], tuple(got[1:])


def cell(step, views, lines, tokens, cotangent, recv, weights, bufs, dims):
    slots, width, ff = dims
    shapes = all_sizes(dims)
    wshapes = weight_sizes(width, ff)
    names = [n for n in shapes if n != "dm"]
    n_in = 2 + len(lines) + 3 + 4
    loads = ("gp", "h", "inv", "ot", "v", "e", "kt", "qt")

    def body(*refs):
        step_ref, views_ref = refs[:2]
        line_hbm = refs[2 : 2 + len(lines)]
        tokens_hbm, cot_hbm, recv_hbm = refs[2 + len(lines) : 5 + len(lines)]
        w_hbm = dict(zip(WEIGHTS, refs[5 + len(lines) : n_in]))
        rest = refs[n_in + len(bufs) :]
        send_hbm, outs_hbm, grads_hbm = rest[:3]
        kept = dict(zip(SAVED + TERMS, rest[3:]))
        rest = rest[3 + len(SAVED + TERMS) :]
        w = dict(zip(WEIGHTS, rest[:4]))
        r = dict(zip(names, rest[4 : 4 + len(names)]))
        x, dm, y, sem, line_sem = rest[4 + len(names) : 9 + len(names)]
        vec = dict(zip(LINES, rest[9 + len(names) :]))
        line_copy = [
            pltpu.make_async_copy(src, vec[n], line_sem.at[i])
            for i, (n, src) in enumerate(zip(LINES, line_hbm))
        ]
        moves = Moves(sem)
        t = step_ref[0]
        lead = lax.axis_index("section") == 0
        run_f = jnp.where(lead, t < 2, t > 0)
        run_b = jnp.where(lead, t == 2, t > 0)
        slot = jnp.where(lead, t % 2, jnp.maximum(t - 1, 0))
        only_b = jnp.logical_and(lead, run_b)
        not_lead = jnp.logical_not(lead)
        token_copy = moves.make("x", tokens_hbm.at[slot, 0], x)
        recv_copy = pltpu.make_async_copy(recv_hbm, x, token_copy_sem(moves, "x"))
        cot_copy = moves.make("dm", cot_hbm.at[slot, 0], dm)
        grad_copy = pltpu.make_async_copy(recv_hbm, dm, token_copy_sem(moves, "dm"))
        w_copy = {n: moves.make("w " + n, w_hbm[n].at[0], w[n]) for n in WEIGHTS}
        l_copy = {n: moves.make("l " + n, kept[n].at[slot], r[n]) for n in loads}
        s_copy = {n: moves.make("s " + n, r[n], kept[n].at[slot]) for n in SAVED}
        b_copy = {n: moves.make("b " + n, r[n], kept[n].at[slot]) for n in TERMS[:4]}
        b_copy["dm"] = moves.make("b dm", dm, kept["dm"].at[slot])
        y_copy = moves.make("y", y, outs_hbm.at[slot])
        g_copy = moves.make("g", x, grads_hbm.at[slot])
        y_send = moves.make("ys", y, send_hbm)
        g_send = moves.make("gs", x, send_hbm)

        @pl.when(run_f)
        def _():
            @pl.when(lead)
            def _():
                token_copy.start()

            @pl.when(not_lead)
            def _():
                recv_copy.start()

            w_copy["qkv"].start()
            for copy in line_copy:
                copy.start()
            for n in WEIGHTS[1:]:
                w_copy[n].start()

            @pl.when(not_lead)
            def _():
                cot_copy.start()

            token_copy.wait()
            for copy in line_copy:
                copy.wait()
            forward(
                x, y, views_ref[slot], vec, w, r,
                lambda n: w_copy[n].wait(), lambda n: s_copy[n].start() if n in s_copy else None,
            )
            y_copy.start()

            @pl.when(lead)
            def _():
                y_send.start()

            @pl.when(not_lead)
            def _():
                cot_copy.wait()

        @pl.when(only_b)
        def _():
            grad_copy.start()
            for copy in line_copy:
                copy.start()
            for n in ("down", "gp", "up", "h", "out", "inv", "ot", "v", "e", "kt", "qt", "qkv"):
                (w_copy if n in w_copy else l_copy)[n].start()
            token_copy.start()
            grad_copy.wait()
            for copy in line_copy:
                copy.wait()
            for n in ("down", "gp", "up", "h"):
                (w_copy if n in w_copy else l_copy)[n].wait()

        @pl.when(run_b)
        def _():
            b_copy["dm"].start()
            backward_mlp(dm, vec, w, r, nothing, lambda n: b_copy[n].start())

            @pl.when(only_b)
            def _():
                for n in ("out", "inv", "ot", "v", "e", "kt", "qt", "qkv"):
                    (w_copy if n in w_copy else l_copy)[n].wait()
                token_copy.wait()

            backward_attention(x, x, vec, w, r, nothing, lambda n: b_copy[n].start())
            g_copy.start()

            @pl.when(not_lead)
            def _():
                g_send.start()

        @pl.when(run_f)
        def _():
            for n in SAVED:
                s_copy[n].wait()
            y_copy.wait()

            @pl.when(lead)
            def _():
                y_send.wait()

        @pl.when(run_b)
        def _():
            for n in TERMS:
                b_copy[n].wait()
            g_copy.wait()

            @pl.when(not_lead)
            def _():
                g_send.wait()

    ins = [(step, "s"), (views, "s")] + [(v, "a") for v in lines]
    ins += [(x, "a") for x in (tokens, cotangent, recv, *weights, *bufs)]
    outs = [((slots, width), BF16, "a")] + [(b.shape, b.dtype, "a") for b in bufs]
    scratch = [pltpu.VMEM(wshapes[n], BF16) for n in WEIGHTS]
    scratch += [pltpu.VMEM(*shapes[n]) for n in names]
    scratch += [pltpu.VMEM((slots, width), BF16)] * 3 + [pltpu.SemaphoreType.DMA((40,))]
    scratch += [pltpu.SemaphoreType.DMA((len(lines),))]
    scratch += [pltpu.VMEM(v.shape, v.dtype) for v in lines]
    got = run(body, ins, outs, scratch, {n_in + i: 1 + i for i in range(len(bufs))}, us=15, limit=BIG)
    return got[0], tuple(got[1:])


def token_copy_sem(moves, name):
    return moves.sem.at[list(moves.made).index(name)]


class Scatter:
    def __init__(self, sem, blocks, keep_hbm, send_hbm):
        self.sem = sem
        self.blocks = blocks
        self.hbm = (keep_hbm, send_hbm)

    def start(self, p, rows, base=0):
        place = jnp.bitwise_xor(p, own_place())
        sem = self.sem.at[base + p]
        src = self.blocks.at[p, rows]
        for side in (0, 1):

            @pl.when(jnp.bitwise_and(place, 1) == side)
            def _():
                pltpu.make_async_copy(src, self.hbm[side].at[place // 2, rows], sem).start()

    def finish(self, rows, base=0):
        for p in range(CUTS):
            src = self.blocks.at[p, rows]
            pltpu.make_async_copy(src, self.hbm[0].at[0, rows], self.sem.at[base + p]).wait()


def with_ones(rows):
    return jnp.concatenate([rows, jnp.ones((16, rows.shape[1]), BF16)], 0)


def own_place():
    return lax.axis_index("dp") if lax.axis_size("dp") == CUTS else 0


def mlp_grads(gain, recv, weights, kept, dims):
    slots, width, ff = dims
    deep = width // 4
    shapes = all_sizes(dims)
    names = ("gp", "h", "du", "dp", "dh", "small")
    given = ("gp", "h", "c", "z", "dm", "du", "dp", "small")
    n_in = 1 + 3 + len(given)

    def body(*refs):
        vec = {"mg": refs[0]}
        recv_hbm, up_hbm, down_hbm = refs[1:4]
        hbm = dict(zip(given, refs[4:n_in]))
        keep, send, sums, dp_hbm, small_hbm, dh_hbm = refs[n_in : n_in + 6]
        rest = refs[n_in + 6 :]
        w = {"up": rest[0], "down": rest[1]}
        r = dict(zip(names, rest[2 : 2 + len(names)]))
        m, z, c, d, turned_ref, blocks, sem, sem2 = rest[2 + len(names) :]
        moves = Moves(sem)
        inner = Moves(sem, 16)
        lead = lax.axis_index("section") == 0
        other = jnp.logical_not(lead)
        half = [slice(0, slots), slice(slots, 2 * slots)]
        m1 = moves.make("m1", hbm["dm"].at[1], m.at[half[1]])
        m1_recv = pltpu.make_async_copy(recv_hbm, m.at[half[1]], sem.at[0])
        d1 = moves.make("d1", hbm["du"].at[1], d.at[half[1]])
        moves.made.pop("d1")
        early = [
            inner.make("down", down_hbm.at[0], w["down"]),
            inner.make("gp", hbm["gp"].at[1], r["gp"]),
            inner.make("up", up_hbm.at[0], w["up"]),
            inner.make("h", hbm["h"].at[1], r["h"]),
        ]
        late = {
            "dp": inner.make("save dp", r["dp"], dp_hbm.at[1]),
            "small": inner.make("save small", r["small"], small_hbm.at[1]),
            "dh": inner.make("save dh", r["dh"], dh_hbm),
        }

        @pl.when(lead)
        def _():
            m1_recv.start()
            for copy in early:
                copy.start()

        @pl.when(other)
        def _():
            m1.start()
            d1.start()

        moves.start("m0", hbm["dm"].at[0], m.at[half[0]])
        for i in (0, 1):
            moves.start("z%d" % i, hbm["z"].at[i], z.at[half[i]])
        for i in (0, 1):
            moves.start("c%d" % i, hbm["c"].at[i], c.at[half[i]])
        moves.start("d0", hbm["du"].at[0], d.at[half[0]])
        scatter = Scatter(sem2, blocks, keep, send)
        upper, lower = slice(0, deep), slice(deep, 2 * deep)
        moves.wait("m1")

        @pl.when(lead)
        def _():
            def done(n):
                if n == "dp":
                    late[n].start()

            r["du"] = d.at[half[1]]
            backward_mlp(m.at[half[1]], vec, w, r, inner.wait, done)
            late["small"].start()
            late["dh"].start()

        moves.wait("m0")
        turned = m[...].T
        sums[4] = dot(jnp.ones((16, 2 * slots), BF16), m[...])[:8]
        turned_ref[:width] = turned
        moves.wait("z0")
        moves.wait("z1")

        def down_part(j, carry):
            cols = pl.ds(pl.multiple_of(j * width, width), width)
            part = dot(turned_ref[:width], z[:, cols]).astype(BF16)
            blocks[pl.ds(4 * j, 4), upper] = part.reshape(4, deep, width)
            for i in range(4):
                scatter.start(4 * j + i, upper)
            return carry

        lax.fori_loop(0, 4, down_part, 0)

        @pl.when(other)
        def _():
            d1.wait()

        moves.finish()
        turned_ref[...] = with_ones(c[...].T)

        def up_part(j, carry):
            cols = pl.ds(pl.multiple_of(j * width, width), width)
            part = dot(turned_ref[...], d[:, cols])
            sums[j] = part[width : width + 8]
            blocks[pl.ds(4 * j, 4), lower] = part[:width].astype(BF16).reshape(4, deep, width)
            for i in range(4):
                scatter.start(4 * j + i, lower, CUTS)
            return carry

        lax.fori_loop(0, 4, up_part, 0)
        scatter.finish(upper)
        scatter.finish(lower, CUTS)

        @pl.when(lead)
        def _():
            for copy in late.values():
                copy.wait()

    half = ((CUTS // 2, 2 * deep, width), BF16, "a")
    ins = [(gain, "v")] + [(recv, "a"), (weights[2], "a"), (weights[3], "a")]
    ins += [(kept[n], "a") for n in given]
    outs = [half, half, ((5, 8, width), F32, "v")]
    outs += [(kept[n].shape, kept[n].dtype, "a") for n in ("dp", "small")]
    outs += [((slots, width), F32, "a")]
    wshapes = weight_sizes(width, ff)
    scratch = [pltpu.VMEM(wshapes["up"], BF16), pltpu.VMEM(wshapes["down"], BF16)]
    scratch += [pltpu.VMEM(*shapes[n]) for n in names]
    scratch += [
        pltpu.VMEM((2 * slots, width), BF16),
        pltpu.VMEM((2 * slots, ff), BF16),
        pltpu.VMEM((2 * slots, width), BF16),
        pltpu.VMEM((2 * slots, ff), BF16),
        pltpu.VMEM((width + 16, 2 * slots), BF16),
        pltpu.VMEM((CUTS, 2 * deep, width), BF16),
        pltpu.SemaphoreType.DMA((24,)),
        pltpu.SemaphoreType.DMA((2 * CUTS,)),
    ]
    return run(body, ins, outs, scratch, {n_in - 2: 3, n_in - 1: 4}, us=12, limit=BIG)


def attention_grads(gain, tokens, weights, kept, dh, grads, sums, dims):
    slots, width, ff = dims
    deep = width // 4
    tall = deep + 16
    shapes = all_sizes(dims)
    names = (
        "dp", "dh", "inv", "ot", "v", "e", "kt", "qt", "s", "ds", "g", "center", "dot", "dqkv",
        "small",
    )
    loads = ("inv", "v", "e", "kt", "qt")
    given = ("a", "ot", "dp", "dqkv", "small") + loads
    n_in = 1 + 6 + len(given)

    def body(*refs):
        vec = {"ag": refs[0]}
        tokens_hbm, out_hbm, qkv_hbm, dh_hbm, grads_in, sums_ref = refs[1:7]
        hbm = dict(zip(given, refs[7:n_in]))
        keep, send, grads_hbm = refs[n_in : n_in + 3]
        rest = refs[n_in + 3 :]
        w = {"out": rest[0], "qkv": rest[1]}
        r = dict(zip(names, rest[2 : 2 + len(names)]))
        x, a, d, o, p, s, turned_ref, lines_ref, blocks, sem, sem2 = rest[2 + len(names) :]
        moves = Moves(sem)
        inner = Moves(sem, 12)
        lead = lax.axis_index("section") == 0
        other = jnp.logical_not(lead)
        half = [slice(0, slots), slice(slots, 2 * slots)]
        place = {
            "dp": lambda i: p.at[half[i]],
            "a": lambda i: a.at[half[i]],
            "ot": lambda i: o.at[:, :, half[i]],
            "dqkv": lambda i: d.at[:, :, :, half[i]],
            "small": lambda i: s.at[i],
        }
        for n in ("dp", "ot", "small"):
            moves.start(n + "1", hbm[n].at[1], place[n](1))
        own = moves.make("dqkv1", hbm["dqkv"].at[1], place["dqkv"](1))
        early = [inner.make("out", out_hbm.at[0], w["out"])]
        early += [inner.make(n, hbm[n].at[1], r[n]) for n in loads]
        early += [
            inner.make("qkv", qkv_hbm.at[0], w["qkv"]),
            inner.make("x", tokens_hbm.at[1, 0], x),
            inner.make("dh", dh_hbm, r["dh"]),
        ]
        g_copy = inner.make("g", x, grads_hbm.at[1])

        @pl.when(other)
        def _():
            own.start()

        @pl.when(lead)
        def _():
            for copy in early:
                copy.start()

        for n in ("a", "dqkv", "ot", "dp", "small"):
            moves.start(n + "0", hbm[n].at[0], place[n](0))
        moves.start("a1", hbm["a"].at[1], place["a"](1))
        for n in ("dp1", "ot1", "small1"):
            moves.wait(n)

        @pl.when(lead)
        def _():
            r.update({n: place[n](1) for n in ("dp", "ot", "dqkv", "small")})

            def wait(n):
                if n == "qkv":
                    inner.wait("x")
                    inner.wait("dh")
                inner.wait(n)

            backward_attention(x, x, vec, w, r, wait, nothing)
            g_copy.start()

        @pl.when(other)
        def _():
            own.wait()

        moves.made.pop("dqkv1")
        moves.finish()
        scatter = Scatter(sem2, blocks, keep, send)
        full, deep_rows = slice(0, tall), slice(0, deep)
        turned_ref[...] = with_ones(a[...].T)

        def qkv_part(j, carry):
            part = dot_nt(turned_ref[...], d[j].reshape(width, 2 * slots))
            lines_ref[j] = part[width : width + 8]
            part = part[:width].astype(BF16).reshape(4, deep, width)
            blocks[pl.ds(4 * j, 4), deep_rows] = part
            return carry

        lax.fori_loop(0, 3, qkv_part, 0)
        part = dot(with_ones(o[...].reshape(width, 2 * slots).astype(BF16)), p[...])
        blocks[12:16, deep_rows] = part[:width].astype(BF16).reshape(4, deep, width)
        both = s[0] + s[1]
        rows = [
            both[A_GAIN_G : A_GAIN_G + 1], both[A_SHIFT_G : A_SHIFT_G + 1],
            lines_ref[0, :1], lines_ref[2, :1],
            part[width : width + 1],
            both[M_GAIN_G : M_GAIN_G + 1], both[M_SHIFT_G : M_SHIFT_G + 1],
            *[sums_ref[i, :1] for i in (4, 0, 1, 2, 3)],
        ]
        for i in range(CUTS):
            line = rows[i] if i < 12 else jnp.zeros((1, width), F32)
            blocks[i, deep:] = jnp.broadcast_to(line, (16, width)).astype(BF16)
            scatter.start(i, full)
        scatter.finish(full)

        @pl.when(lead)
        def _():
            g_copy.wait()

    ins = [(gain, "v")] + [(tokens, "a"), (weights[1], "a"), (weights[0], "a")]
    ins += [(dh, "a"), (grads, "a"), (sums, "v")]
    ins += [(kept[n], "a") for n in given]
    half = ((CUTS // 2, tall, width), BF16, "a")
    outs = [half, half, (grads.shape, grads.dtype, "a")]
    wshapes = weight_sizes(width, ff)
    scratch = [pltpu.VMEM(wshapes["out"], BF16), pltpu.VMEM(wshapes["qkv"], BF16)]
    scratch += [pltpu.VMEM(*shapes[n]) for n in names]
    scratch += [
        pltpu.VMEM((slots, width), BF16),
        pltpu.VMEM((2 * slots, width), BF16),
        pltpu.VMEM((3, HEADS, HEAD, 2 * slots), BF16),
        pltpu.VMEM((HEADS, HEAD, 2 * slots), F32),
        pltpu.VMEM((2 * slots, width), BF16),
        pltpu.VMEM((2, 8, width), F32),
        pltpu.VMEM((width + 16, 2 * slots), BF16),
        pltpu.VMEM((3, 8, width), F32),
    ]
    scratch += [
        pltpu.VMEM((CUTS, tall, width), BF16),
        pltpu.SemaphoreType.DMA((24,)),
        pltpu.SemaphoreType.DMA((CUTS,)),
    ]
    return run(body, ins, outs, scratch, {1 + 4: 2}, us=12, limit=MID)


def block(own, other, p):
    place = jnp.bitwise_xor(p, own_place())
    mine = own[place // 2]
    theirs = other[place // 2]
    odd = jnp.bitwise_and(place, 1)
    return jnp.where(odd == 1, theirs, mine).astype(F32)


def mlp_out(own, other, dims):
    slots, width, ff = dims
    deep = width // 4

    def body(own_ref, other_ref, down, up, token):
        token[...] = jnp.zeros((8, LANES), F32)
        for j in range(4):
            part = [block(own_ref, other_ref, 4 * j + i) for i in range(4)]
            down[0, j * width : (j + 1) * width, :] = jnp.concatenate(
                [v[:deep] for v in part], 0
            ).T
            up[0, :, j * width : (j + 1) * width] = jnp.concatenate([v[deep:] for v in part], 0)

    outs = [((1, ff, width), F32, "v"), ((1, width, ff), F32, "v"), ((8, LANES), F32, "v")]
    return run(body, [(own, "v"), (other, "v")], outs, [], us=4)


def attention_out(own, other, dims):
    slots, width, ff = dims
    deep = width // 4

    def body(own_ref, other_ref, qkv, out, *lines):
        for p in range(CUTS):
            j, i = p // 4, p % 4
            got = block(own_ref, other_ref, p)
            if j < 3:
                qkv[0, i * deep : (i + 1) * deep, j * width : (j + 1) * width] = got[:deep]
            else:
                out[0, i * deep : (i + 1) * deep, :] = got[:deep]
            if p < 8:
                lines[p][...] = got[deep : deep + 1]
            elif p < 12:
                lines[8][:, (p - 8) * width : (p - 7) * width] = got[deep : deep + 1]

    outs = [((1, width, 3 * width), F32, "v"), ((1, width, width), F32, "v")]
    outs += [((1, width), F32, "v")] * 8 + [((1, ff), F32, "v")]
    return run(body, [(own, "v"), (other, "v")], outs, [], us=3)


def swapped(x, bits):
    return lax.ppermute(x, "dp", [(i, i ^ bits) for i in range(CUTS)])


def added(*parts):
    total = parts[0].astype(F32)
    for x in parts[1:]:
        total = total + x.astype(F32)
    return total.astype(BF16)


def tied(token, *xs):
    return lax.optimization_barrier((token, *xs))[1:]


def square_send(u):
    return [swapped(u[:, j], 2 * j) for j in (1, 2, 3)]


def square_gather(u):
    return [swapped(u, 2 * j) for j in (1, 2, 3)]


def shards(
    tokens, cotangent, views, attn_gain, attn_shift, qkv_weight, query_bias, value_bias,
    out_weight, out_bias, mlp_gain, mlp_shift, up_weight, up_bias, down_weight, down_bias,
):
    dims = (tokens.shape[2], tokens.shape[3], up_bias.shape[1])
    weights = (qkv_weight, out_weight, up_weight, down_weight)
    lines = (
        attn_gain, attn_shift, query_bias, value_bias, out_bias, mlp_gain, mlp_shift, down_bias,
        up_bias,
    )

    counts = views[:, 0]

    def advance(t, carry):
        recv, bufs = carry
        step = jnp.reshape(t, (1,))
        send, bufs = cell(step, counts, lines, tokens, cotangent, recv, weights, bufs, dims)
        return lax.ppermute(send, "section", [(0, 1), (1, 0)]), bufs

    recv, bufs = lax.fori_loop(0, STEPS, advance, blank(dims))
    outs, grads = bufs[:2]
    kept = dict(zip(SAVED + TERMS, bufs[2:]))
    m_keep, m_send, sums, kept["dp"], kept["small"], dh = mlp_grads(
        mlp_gain, recv, weights, kept, dims
    )
    if lax.axis_size("dp") != CUTS:
        a_keep, a_send, grads = attention_grads(attn_gain, tokens, weights, kept, dh, grads, sums, dims)
        m, m_other, a, a_other = lax.psum((m_keep, m_send, a_keep, a_send), "dp")
        g_down, g_up, _ = mlp_out(m, m_other, dims)
    else:
        m = added(m_keep, swapped(m_send, 1)).reshape(2, 4, *m_keep.shape[1:])
        m1 = square_send(m)
        (dh,) = tied(m, dh)
        a_keep, a_send, grads = attention_grads(attn_gain, tokens, weights, kept, dh, grads, sums, dims)
        a_got = jnp.concatenate([swapped(v, 1) for v in jnp.split(a_send, 2)], 0)
        m1 = tied(a_keep, *m1)
        m = added(m[:, 0], *m1)
        m2 = swapped(m, 8)
        (a_got,) = tied(m, a_got)
        a = added(a_keep, a_got).reshape(2, 4, *a_keep.shape[1:])
        a1 = square_send(a)
        m2, *a1 = lax.optimization_barrier((m2, *a1))
        m = added(m, m2[::-1])
        m1 = square_gather(m)
        a = added(a[:, 0], *a1)
        a2 = swapped(a, 8)
        (a2,) = tied(m, a2)
        a = added(a, a2[::-1])
        a1 = square_gather(a)
        m1 = tied(a, *m1)
        m = jnp.stack([m, *m1], 1).reshape(8, *m.shape[1:])
        g_down, g_up, token = mlp_out(m, swapped(m, 1), dims)
        a1 = tied(token, *a1)
        a = jnp.stack([a, *a1], 1).reshape(8, *a.shape[1:])
        a_other = swapped(a, 1)
    g_qkv, g_out, *rows = attention_out(a, a_other, dims)
    g_ag, g_as, g_qb, g_vb, g_ob, g_mg, g_ms, g_db, g_ub = rows
    return (
        outs[None, :, None], grads[None, :, None], g_ag, g_as, g_qkv, g_qb, g_vb, g_out, g_ob,
        g_mg, g_ms, g_up, g_ub, g_down, g_db,
    )


def solution(mesh):
    scene = P(None, "dp", None, None)
    line = P("section", None)
    table = P("section", None, None)
    kept = P("section", None, "dp", None, None)
    kinds = (line, line, table, line, line, table, line, line, line, table, line, table, line)
    return jax.shard_map(
        shards,
        mesh=mesh,
        in_specs=(scene, scene, P(None, "dp")) + kinds,
        out_specs=(kept, kept) + kinds,
        check_vma=False,
    )
```

```python
import jax
import jax.numpy as jnp
from jax import lax
from jax.experimental import pallas as pl
from jax.experimental.pallas import tpu as pltpu
from jax.sharding import PartitionSpec as P

HEADS = 6
HEAD = 64
PATCHES = 64
EPSILON = 1e-06
MASKED = -1e30
LANES = 128
CUTS = 16
F32 = jnp.float32
BF16 = jnp.bfloat16
VMEM_LIMIT = 16 * 2**20
BIG = 52 * 2**20
MID = 52 * 2**20


def dot(a, b):
    return lax.dot_general(a, b, (((1,), (0,)), ((), ())), preferred_element_type=F32)


def dot_nt(a, b):
    return lax.dot_general(a, b, (((1,), (1,)), ((), ())), preferred_element_type=F32)


def unit_rows(values):
    center = values - jnp.mean(values, -1, keepdims=True)
    spread = jnp.mean(center * center, -1, keepdims=True)
    scale = lax.rsqrt(spread + EPSILON)
    return center * scale, scale


def row(vec, name):
    return vec[name][...].astype(F32)


LINES = ("ag", "as", "qb", "vb", "ob", "mg", "ms", "db", "ub")
CHUNK = 256
LOG2E = 1.4426950408889634
WIDE = 256


def padded(rows, odd):
    zero = jnp.zeros_like(rows)
    return jnp.concatenate([zero, rows] if odd else [rows, zero], 0)


def forward(x_ref, y_ref, count, vec, w, r, wait, done):
    slots, width = x_ref.shape
    ub = row(vec, "ub")
    ff = ub.shape[1]

    unit, _ = unit_rows(x_ref[...].astype(F32))
    a = (unit * row(vec, "ag") + row(vec, "as")).astype(BF16)
    r["a"][...] = a
    wait("qkv")
    q = dot(a, w["qkv"][:, :width]) + row(vec, "qb")
    r["qt"][...] = (q * HEAD**-0.5).astype(BF16).T.reshape(HEADS, HEAD, slots)
    k = dot(a, w["qkv"][:, width : 2 * width]).astype(BF16)
    r["kt"][...] = k.T.reshape(HEADS, HEAD, slots)
    v = (dot(a, w["qkv"][:, 2 * width :]) + row(vec, "vb")).astype(BF16)
    r["vt"][...] = v.T.reshape(HEADS, HEAD, slots)
    for p in range(HEADS // 2):
        r["k"][p] = k[:, p * 2 * HEAD : (p + 1) * 2 * HEAD]
        r["v"][p] = v[:, p * 2 * HEAD : (p + 1) * 2 * HEAD]
    for n in ("a", "qt", "k", "kt", "v"):
        done(n)
    groups = slots // PATCHES
    shift = [jnp.where(g < count, 0.0, MASKED).astype(F32) for g in range(groups)]

    last = HEADS - 1

    def scores(h, odd):
        r["s"][odd] = dot(r["k"][h // 2], padded(r["qt"][h], odd))

    def soften(h, odd):
        s_ref = r["s"].at[odd]
        for c in range(slots // WIDE):
            cols = slice(c * WIDE, (c + 1) * WIDE)
            peak = None
            for g in range(groups):
                block = s_ref[g * PATCHES : (g + 1) * PATCHES, cols]
                top = jnp.max(block.reshape(PATCHES // 8, 8, WIDE), 0)
                top = top if g < 2 else top + shift[g]
                peak = top if g == 0 else jnp.maximum(peak, top)
            peak = jnp.max(peak, 0, keepdims=True)
            acc = jnp.zeros((8, WIDE), F32)
            for g in range(groups):
                block = s_ref[g * PATCHES : (g + 1) * PATCHES, cols]
                e = jnp.exp(block - (peak - shift[g]))
                acc = acc + jnp.sum(e.reshape(PATCHES // 8, 8, WIDE), 0)
                r["e"][h, g * PATCHES : (g + 1) * PATCHES, cols] = e.astype(BF16)
            r["inv"][h, :, cols] = 1.0 / jnp.sum(acc, 0, keepdims=True)

    def mix(h):
        r["ot"][h] = dot(r["vt"][h], r["e"][h]) * r["inv"][h]

    def pair(i):
        h = 2 * i
        scores(h + 1, 1)
        soften(h, 0)
        if h:
            mix(h - 1)
        if h + 2 < HEADS:
            scores(h + 2, 0)
        soften(h + 1, 1)
        mix(h)

    scores(0, 0)
    for i in range(HEADS // 2):
        pair(i)
    mix(last)
    for n in ("e", "inv", "ot"):
        done(n)
    wait("out")
    o = r["ot"][...].reshape(width, slots).astype(BF16).T
    hidden = x_ref[...].astype(F32) + dot(o, w["out"][...]) + row(vec, "ob")
    r["h"][...] = hidden
    done("h")
    unit, _ = unit_rows(hidden)
    c = (unit * row(vec, "mg") + row(vec, "ms")).astype(BF16)
    r["c"][...] = c
    done("c")
    wait("up")
    for f in range(0, ff, CHUNK):
        cols = slice(f, f + CHUNK)
        u = dot(c, w["up"][:, cols]) + ub[:, cols]
        t = u * 0.5**0.5
        phi = 0.5 + 0.5 * lax.erf(t)
        bell = jnp.exp2(t * t * -LOG2E)
        r["z"][:, cols] = (u * phi).astype(BF16)
        r["gp"][:, cols] = (phi + u * 0.3989422804014327 * bell).astype(BF16)
    done("z")
    done("gp")
    wait("down")
    y_ref[...] = (r["h"][...] + dot(r["z"][...], w["down"][...]) + row(vec, "db")).astype(BF16)


def nothing(name):
    pass


def sizes(slots, width, ff):
    turned = ((HEADS, HEAD, slots), BF16)
    pairs = ((HEADS // 2, slots, 2 * HEAD), BF16)
    return dict(
        a=((slots, width), BF16),
        qt=turned,
        k=pairs,
        kt=turned,
        v=pairs,
        vt=turned,
        s=((2, slots, slots), F32),
        e=((HEADS, slots, slots), BF16),
        inv=((HEADS, 1, slots), F32),
        ot=((HEADS, HEAD, slots), F32),
        h=((slots, width), F32),
        c=((slots, width), BF16),
        z=((slots, ff), BF16),
        gp=((slots, ff), BF16),
    )


def norm_back(grad, gain, unit, scale):
    t = grad * gain
    inner = jnp.mean(t, -1, keepdims=True)
    along = jnp.mean(t * unit, -1, keepdims=True)
    return scale * (t - inner - unit * along)


M_GAIN_G, M_SHIFT_G, A_GAIN_G, A_SHIFT_G = range(4)


def backward_mlp(grad_ref, vec, w, r, wait, done):
    slots, width = grad_ref.shape
    ff = r["du"].shape[1]
    wait("down")
    wait("gp")
    low = grad_ref[...]
    for f in range(0, ff, CHUNK):
        cols = slice(f, f + CHUNK)
        dz = dot_nt(low, w["down"][cols, :])
        r["du"][:, cols] = (dz * r["gp"][:, cols].astype(F32)).astype(BF16)
    done("du")
    wait("up")
    dc = dot_nt(r["du"][...], w["up"][...])
    wait("h")
    unit, scale = unit_rows(r["h"][...])
    r["small"][M_GAIN_G : M_GAIN_G + 1, :] = jnp.sum(dc * unit, 0, keepdims=True)
    r["small"][M_SHIFT_G : M_SHIFT_G + 1, :] = jnp.sum(dc, 0, keepdims=True)
    dh = low.astype(F32) + norm_back(dc, row(vec, "mg"), unit, scale)
    r["dh"][...] = dh
    r["dp"][...] = dh.astype(BF16)
    done("dp")


def backward_attention(x_ref, g_ref, vec, w, r, wait, done):
    slots, width = x_ref.shape
    wait("out")
    dot_t = dot_nt(w["out"][...], r["dp"][...])
    r["dot"][...] = dot_t.reshape(HEADS, HEAD, slots)

    last = HEADS - 1
    for n in ("inv", "ot", "v", "e", "kt", "qt"):
        wait(n)

    def spread(h, odd):
        g = (r["dot"][h] * r["inv"][h]).astype(BF16)
        r["g"][odd] = g
        r["center"][odd] = jnp.sum(g.astype(F32) * r["ot"][h], 0, keepdims=True)
        r["s"][odd] = dot(r["v"][h // 2], padded(g, odd))

    def weigh(h, odd):
        s_ref = r["s"].at[odd]
        for c in range(slots // WIDE):
            cols = slice(c * WIDE, (c + 1) * WIDE)
            center = r["center"][odd, :, cols]
            for b in range(0, slots, PATCHES):
                block = s_ref[b : b + PATCHES, cols] - center
                r["ds"][odd, b : b + PATCHES, cols] = (
                    block * r["e"][h, b : b + PATCHES, cols].astype(F32)
                ).astype(BF16)

    def gather(h, odd):
        ds = r["ds"][odd]
        r["dqkv"][0, h] = (dot(r["kt"][h], ds) * HEAD**-0.5).astype(BF16)
        r["dqkv"][1, h] = dot_nt(r["qt"][h], ds).astype(BF16)

    def gather_v(h, odd):
        r["dqkv"][2, h] = dot_nt(r["g"][odd], r["e"][h]).astype(BF16)

    def pair(i):
        h = 2 * i
        gather_v(h, 0)
        spread(h + 1, 1)
        weigh(h, 0)
        if h:
            gather(h - 1, 1)
        gather_v(h + 1, 1)
        if h + 2 < HEADS:
            spread(h + 2, 0)
        weigh(h + 1, 1)
        gather(h, 0)

    spread(0, 0)
    for i in range(HEADS // 2):
        pair(i)
    gather(last, 1)
    done("dqkv")

    wait("qkv")
    da = dot(w["qkv"][...], r["dqkv"][...].reshape(3 * width, slots)).T
    unit, scale = unit_rows(x_ref[...].astype(F32))
    r["small"][A_GAIN_G : A_GAIN_G + 1, :] = jnp.sum(da * unit, 0, keepdims=True)
    r["small"][A_SHIFT_G : A_SHIFT_G + 1, :] = jnp.sum(da, 0, keepdims=True)
    done("small")
    g_ref[...] = (r["dh"][...] + norm_back(da, row(vec, "ag"), unit, scale)).astype(BF16)


def back_sizes(slots, width, ff):
    return dict(
        du=((slots, ff), BF16),
        dh=((slots, width), F32),
        dp=((slots, width), BF16),
        dot=((HEADS, HEAD, slots), F32),
        ds=((2, slots, slots), BF16),
        g=((2, HEAD, slots), BF16),
        center=((2, 1, slots), F32),
        dqkv=((3, HEADS, HEAD, slots), BF16),
        small=((8, width), F32),
    )


WEIGHTS = ("qkv", "out", "up", "down")
SAVED = ("a", "qt", "kt", "v", "e", "inv", "ot", "h", "c", "z", "gp")
TERMS = ("du", "dp", "dqkv", "small", "dm")
STEPS = 3


def run(body, ins, outs, scratch, aliases=None, us=1, limit=VMEM_LIMIT):
    space = {"s": pltpu.SMEM, "v": pltpu.VMEM, "a": pl.ANY}
    return pl.pallas_call(
        body,
        out_shape=[jax.ShapeDtypeStruct(s, t) for s, t, _ in outs],
        in_specs=[pl.BlockSpec(memory_space=space[k]) for _, k in ins],
        out_specs=[pl.BlockSpec(memory_space=space[k]) for _, _, k in outs],
        scratch_shapes=scratch,
        input_output_aliases=aliases or {},
        compiler_params=pltpu.CompilerParams(vmem_limit_bytes=limit),
        cost_estimate=pl.CostEstimate(
            flops=us * 10**9, bytes_accessed=us * 2 * 10**6, transcendentals=0
        ),
    )(*[x for x, _ in ins])


def weight_sizes(width, ff):
    return dict(qkv=(width, 3 * width), out=(width, width), up=(width, ff), down=(ff, width))


def all_sizes(dims):
    slots, width, ff = dims
    return {**sizes(*dims), **back_sizes(*dims), "dm": ((slots, width), BF16)}


class Moves:
    def __init__(self, sem, used=0):
        self.sem = sem
        self.used = used
        self.made = {}

    def make(self, name, src, dst):
        self.made[name] = pltpu.make_async_copy(src, dst, self.sem.at[self.used])
        self.used += 1
        return self.made[name]

    def start(self, name, src, dst):
        self.make(name, src, dst).start()

    def wait(self, name):
        if name in self.made:
            self.made.pop(name).wait()

    def finish(self):
        for name in list(self.made):
            self.wait(name)


def blank(dims):
    slots, width, _ = dims
    shapes = all_sizes(dims)
    outs = [((slots, width), BF16, "a")] + [((2, slots, width), BF16, "a")] * 2
    outs += [((2, *shapes[n][0]), shapes[n][1], "a") for n in SAVED + TERMS]

    def body(*refs):
        pass

    got = run(body, [], outs, [])
    return got[0], tuple(got[1:])


def cell(step, views, lines, tokens, cotangent, recv, weights, bufs, dims):
    slots, width, ff = dims
    shapes = all_sizes(dims)
    wshapes = weight_sizes(width, ff)
    names = [n for n in shapes if n != "dm"]
    n_in = 2 + len(lines) + 3 + 4
    loads = ("gp", "h", "inv", "ot", "v", "e", "kt", "qt")

    def body(*refs):
        step_ref, views_ref = refs[:2]
        line_hbm = refs[2 : 2 + len(lines)]
        tokens_hbm, cot_hbm, recv_hbm = refs[2 + len(lines) : 5 + len(lines)]
        w_hbm = dict(zip(WEIGHTS, refs[5 + len(lines) : n_in]))
        rest = refs[n_in + len(bufs) :]
        send_hbm, outs_hbm, grads_hbm = rest[:3]
        kept = dict(zip(SAVED + TERMS, rest[3:]))
        rest = rest[3 + len(SAVED + TERMS) :]
        w = dict(zip(WEIGHTS, rest[:4]))
        r = dict(zip(names, rest[4 : 4 + len(names)]))
        x, dm, y, sem, line_sem = rest[4 + len(names) : 9 + len(names)]
        vec = dict(zip(LINES, rest[9 + len(names) :]))
        line_copy = [
            pltpu.make_async_copy(src, vec[n], line_sem.at[i])
            for i, (n, src) in enumerate(zip(LINES, line_hbm))
        ]
        moves = Moves(sem)
        t = step_ref[0]
        lead = lax.axis_index("section") == 0
        run_f = jnp.where(lead, t < 2, t > 0)
        run_b = jnp.where(lead, t == 2, t > 0)
        slot = jnp.where(lead, t % 2, jnp.maximum(t - 1, 0))
        only_b = jnp.logical_and(lead, run_b)
        not_lead = jnp.logical_not(lead)
        token_copy = moves.make("x", tokens_hbm.at[slot, 0], x)
        recv_copy = pltpu.make_async_copy(recv_hbm, x, token_copy_sem(moves, "x"))
        cot_copy = moves.make("dm", cot_hbm.at[slot, 0], dm)
        grad_copy = pltpu.make_async_copy(recv_hbm, dm, token_copy_sem(moves, "dm"))
        w_copy = {n: moves.make("w " + n, w_hbm[n].at[0], w[n]) for n in WEIGHTS}
        l_copy = {n: moves.make("l " + n, kept[n].at[slot], r[n]) for n in loads}
        s_copy = {n: moves.make("s " + n, r[n], kept[n].at[slot]) for n in SAVED}
        b_copy = {n: moves.make("b " + n, r[n], kept[n].at[slot]) for n in TERMS[:4]}
        b_copy["dm"] = moves.make("b dm", dm, kept["dm"].at[slot])
        y_copy = moves.make("y", y, outs_hbm.at[slot])
        g_copy = moves.make("g", x, grads_hbm.at[slot])
        y_send = moves.make("ys", y, send_hbm)
        g_send = moves.make("gs", x, send_hbm)

        @pl.when(run_f)
        def _():
            @pl.when(lead)
            def _():
                token_copy.start()

            @pl.when(not_lead)
            def _():
                recv_copy.start()

            w_copy["qkv"].start()
            for copy in line_copy:
                copy.start()
            for n in WEIGHTS[1:]:
                w_copy[n].start()

            @pl.when(not_lead)
            def _():
                cot_copy.start()

            token_copy.wait()
            for copy in line_copy:
                copy.wait()
            forward(
                x, y, views_ref[slot], vec, w, r,
                lambda n: w_copy[n].wait(), lambda n: s_copy[n].start() if n in s_copy else None,
            )
            y_copy.start()

            @pl.when(lead)
            def _():
                y_send.start()

            @pl.when(not_lead)
            def _():
                cot_copy.wait()

        @pl.when(only_b)
        def _():
            grad_copy.start()
            for copy in line_copy:
                copy.start()
            for n in ("down", "gp", "up", "h", "out", "inv", "ot", "v", "e", "kt", "qt", "qkv"):
                (w_copy if n in w_copy else l_copy)[n].start()
            token_copy.start()
            grad_copy.wait()
            for copy in line_copy:
                copy.wait()
            for n in ("down", "gp", "up", "h"):
                (w_copy if n in w_copy else l_copy)[n].wait()

        @pl.when(run_b)
        def _():
            b_copy["dm"].start()
            backward_mlp(dm, vec, w, r, nothing, lambda n: b_copy[n].start())

            @pl.when(only_b)
            def _():
                for n in ("out", "inv", "ot", "v", "e", "kt", "qt", "qkv"):
                    (w_copy if n in w_copy else l_copy)[n].wait()
                token_copy.wait()

            backward_attention(x, x, vec, w, r, nothing, lambda n: b_copy[n].start())
            g_copy.start()

            @pl.when(not_lead)
            def _():
                g_send.start()

        @pl.when(run_f)
        def _():
            for n in SAVED:
                s_copy[n].wait()
            y_copy.wait()

            @pl.when(lead)
            def _():
                y_send.wait()

        @pl.when(run_b)
        def _():
            for n in TERMS:
                b_copy[n].wait()
            g_copy.wait()

            @pl.when(not_lead)
            def _():
                g_send.wait()

    ins = [(step, "s"), (views, "s")] + [(v, "a") for v in lines]
    ins += [(x, "a") for x in (tokens, cotangent, recv, *weights, *bufs)]
    outs = [((slots, width), BF16, "a")] + [(b.shape, b.dtype, "a") for b in bufs]
    scratch = [pltpu.VMEM(wshapes[n], BF16) for n in WEIGHTS]
    scratch += [pltpu.VMEM(*shapes[n]) for n in names]
    scratch += [pltpu.VMEM((slots, width), BF16)] * 3 + [pltpu.SemaphoreType.DMA((40,))]
    scratch += [pltpu.SemaphoreType.DMA((len(lines),))]
    scratch += [pltpu.VMEM(v.shape, v.dtype) for v in lines]
    got = run(body, ins, outs, scratch, {n_in + i: 1 + i for i in range(len(bufs))}, us=15, limit=BIG)
    return got[0], tuple(got[1:])


def token_copy_sem(moves, name):
    return moves.sem.at[list(moves.made).index(name)]


class Scatter:
    def __init__(self, sem, blocks, keep_hbm, send_hbm):
        self.sem = sem
        self.blocks = blocks
        self.hbm = (keep_hbm, send_hbm)

    def start(self, p, rows, base=0):
        place = jnp.bitwise_xor(p, own_place())
        sem = self.sem.at[base + p]
        src = self.blocks.at[p, rows]
        for side in (0, 1):

            @pl.when(jnp.bitwise_and(place, 1) == side)
            def _():
                pltpu.make_async_copy(src, self.hbm[side].at[place // 2, rows], sem).start()

    def finish(self, rows, base=0):
        for p in range(CUTS):
            src = self.blocks.at[p, rows]
            pltpu.make_async_copy(src, self.hbm[0].at[0, rows], self.sem.at[base + p]).wait()


def with_ones(rows):
    return jnp.concatenate([rows, jnp.ones((16, rows.shape[1]), BF16)], 0)


def own_place():
    return lax.axis_index("dp") if lax.axis_size("dp") == CUTS else 0


def mlp_grads(gain, recv, weights, kept, dims):
    slots, width, ff = dims
    deep = width // 4
    shapes = all_sizes(dims)
    names = ("gp", "h", "du", "dp", "dh", "small")
    given = ("gp", "h", "c", "z", "dm", "du", "dp", "small")
    n_in = 1 + 3 + len(given)

    def body(*refs):
        vec = {"mg": refs[0]}
        recv_hbm, up_hbm, down_hbm = refs[1:4]
        hbm = dict(zip(given, refs[4:n_in]))
        keep, send, sums, dp_hbm, small_hbm, dh_hbm = refs[n_in : n_in + 6]
        rest = refs[n_in + 6 :]
        w = {"up": rest[0], "down": rest[1]}
        r = dict(zip(names, rest[2 : 2 + len(names)]))
        m, z, c, d, turned_ref, blocks, sem, sem2 = rest[2 + len(names) :]
        moves = Moves(sem)
        inner = Moves(sem, 16)
        lead = lax.axis_index("section") == 0
        other = jnp.logical_not(lead)
        half = [slice(0, slots), slice(slots, 2 * slots)]
        m1 = moves.make("m1", hbm["dm"].at[1], m.at[half[1]])
        m1_recv = pltpu.make_async_copy(recv_hbm, m.at[half[1]], sem.at[0])
        d1 = moves.make("d1", hbm["du"].at[1], d.at[half[1]])
        moves.made.pop("d1")
        early = [
            inner.make("down", down_hbm.at[0], w["down"]),
            inner.make("gp", hbm["gp"].at[1], r["gp"]),
            inner.make("up", up_hbm.at[0], w["up"]),
            inner.make("h", hbm["h"].at[1], r["h"]),
        ]
        late = {
            "dp": inner.make("save dp", r["dp"], dp_hbm.at[1]),
            "small": inner.make("save small", r["small"], small_hbm.at[1]),
            "dh": inner.make("save dh", r["dh"], dh_hbm),
        }

        @pl.when(lead)
        def _():
            m1_recv.start()
            for copy in early:
                copy.start()

        @pl.when(other)
        def _():
            m1.start()
            d1.start()

        moves.start("m0", hbm["dm"].at[0], m.at[half[0]])
        for i in (0, 1):
            moves.start("z%d" % i, hbm["z"].at[i], z.at[half[i]])
        for i in (0, 1):
            moves.start("c%d" % i, hbm["c"].at[i], c.at[half[i]])
        moves.start("d0", hbm["du"].at[0], d.at[half[0]])
        scatter = Scatter(sem2, blocks, keep, send)
        upper, lower = slice(0, deep), slice(deep, 2 * deep)
        moves.wait("m1")

        @pl.when(lead)
        def _():
            def done(n):
                if n == "dp":
                    late[n].start()

            r["du"] = d.at[half[1]]
            backward_mlp(m.at[half[1]], vec, w, r, inner.wait, done)
            late["small"].start()
            late["dh"].start()

        moves.wait("m0")
        turned = m[...].T
        sums[4] = dot(jnp.ones((16, 2 * slots), BF16), m[...])[:8]
        turned_ref[:width] = turned
        moves.wait("z0")
        moves.wait("z1")

        def down_part(j, carry):
            cols = pl.ds(pl.multiple_of(j * width, width), width)
            part = dot(turned_ref[:width], z[:, cols]).astype(BF16)
            blocks[pl.ds(4 * j, 4), upper] = part.reshape(4, deep, width)
            for i in range(4):
                scatter.start(4 * j + i, upper)
            return carry

        lax.fori_loop(0, 4, down_part, 0)

        @pl.when(other)
        def _():
            d1.wait()

        moves.finish()
        turned_ref[...] = with_ones(c[...].T)

        def up_part(j, carry):
            cols = pl.ds(pl.multiple_of(j * width, width), width)
            part = dot(turned_ref[...], d[:, cols])
            sums[j] = part[width : width + 8]
            blocks[pl.ds(4 * j, 4), lower] = part[:width].astype(BF16).reshape(4, deep, width)
            for i in range(4):
                scatter.start(4 * j + i, lower, CUTS)
            return carry

        lax.fori_loop(0, 4, up_part, 0)
        scatter.finish(upper)
        scatter.finish(lower, CUTS)

        @pl.when(lead)
        def _():
            for copy in late.values():
                copy.wait()

    half = ((CUTS // 2, 2 * deep, width), BF16, "a")
    ins = [(gain, "v")] + [(recv, "a"), (weights[2], "a"), (weights[3], "a")]
    ins += [(kept[n], "a") for n in given]
    outs = [half, half, ((5, 8, width), F32, "v")]
    outs += [(kept[n].shape, kept[n].dtype, "a") for n in ("dp", "small")]
    outs += [((slots, width), F32, "a")]
    wshapes = weight_sizes(width, ff)
    scratch = [pltpu.VMEM(wshapes["up"], BF16), pltpu.VMEM(wshapes["down"], BF16)]
    scratch += [pltpu.VMEM(*shapes[n]) for n in names]
    scratch += [
        pltpu.VMEM((2 * slots, width), BF16),
        pltpu.VMEM((2 * slots, ff), BF16),
        pltpu.VMEM((2 * slots, width), BF16),
        pltpu.VMEM((2 * slots, ff), BF16),
        pltpu.VMEM((width + 16, 2 * slots), BF16),
        pltpu.VMEM((CUTS, 2 * deep, width), BF16),
        pltpu.SemaphoreType.DMA((24,)),
        pltpu.SemaphoreType.DMA((2 * CUTS,)),
    ]
    return run(body, ins, outs, scratch, {n_in - 2: 3, n_in - 1: 4}, us=12, limit=BIG)


def attention_grads(gain, tokens, weights, kept, dh, grads, sums, dims):
    slots, width, ff = dims
    deep = width // 4
    tall = deep + 16
    shapes = all_sizes(dims)
    names = (
        "dp", "dh", "inv", "ot", "v", "e", "kt", "qt", "s", "ds", "g", "center", "dot", "dqkv",
        "small",
    )
    loads = ("inv", "v", "e", "kt", "qt")
    given = ("a", "ot", "dp", "dqkv", "small") + loads
    n_in = 1 + 6 + len(given)

    def body(*refs):
        vec = {"ag": refs[0]}
        tokens_hbm, out_hbm, qkv_hbm, dh_hbm, grads_in, sums_ref = refs[1:7]
        hbm = dict(zip(given, refs[7:n_in]))
        keep, send, grads_hbm = refs[n_in : n_in + 3]
        rest = refs[n_in + 3 :]
        w = {"out": rest[0], "qkv": rest[1]}
        r = dict(zip(names, rest[2 : 2 + len(names)]))
        x, a, d, o, p, s, turned_ref, lines_ref, blocks, sem, sem2 = rest[2 + len(names) :]
        moves = Moves(sem)
        inner = Moves(sem, 12)
        lead = lax.axis_index("section") == 0
        other = jnp.logical_not(lead)
        half = [slice(0, slots), slice(slots, 2 * slots)]
        place = {
            "dp": lambda i: p.at[half[i]],
            "a": lambda i: a.at[half[i]],
            "ot": lambda i: o.at[:, :, half[i]],
            "dqkv": lambda i: d.at[:, :, :, half[i]],
            "small": lambda i: s.at[i],
        }
        for n in ("dp", "ot", "small"):
            moves.start(n + "1", hbm[n].at[1], place[n](1))
        own = moves.make("dqkv1", hbm["dqkv"].at[1], place["dqkv"](1))
        early = [inner.make("out", out_hbm.at[0], w["out"])]
        early += [inner.make(n, hbm[n].at[1], r[n]) for n in loads]
        early += [
            inner.make("qkv", qkv_hbm.at[0], w["qkv"]),
            inner.make("x", tokens_hbm.at[1, 0], x),
            inner.make("dh", dh_hbm, r["dh"]),
        ]
        g_copy = inner.make("g", x, grads_hbm.at[1])

        @pl.when(other)
        def _():
            own.start()

        @pl.when(lead)
        def _():
            for copy in early:
                copy.start()

        for n in ("a", "dqkv", "ot", "dp", "small"):
            moves.start(n + "0", hbm[n].at[0], place[n](0))
        moves.start("a1", hbm["a"].at[1], place["a"](1))
        for n in ("dp1", "ot1", "small1"):
            moves.wait(n)

        @pl.when(lead)
        def _():
            r.update({n: place[n](1) for n in ("dp", "ot", "dqkv", "small")})

            def wait(n):
                if n == "qkv":
                    inner.wait("x")
                    inner.wait("dh")
                inner.wait(n)

            backward_attention(x, x, vec, w, r, wait, nothing)
            g_copy.start()

        @pl.when(other)
        def _():
            own.wait()

        moves.made.pop("dqkv1")
        moves.finish()
        scatter = Scatter(sem2, blocks, keep, send)
        full, deep_rows = slice(0, tall), slice(0, deep)
        turned_ref[...] = with_ones(a[...].T)

        def qkv_part(j, carry):
            part = dot_nt(turned_ref[...], d[j].reshape(width, 2 * slots))
            lines_ref[j] = part[width : width + 8]
            part = part[:width].astype(BF16).reshape(4, deep, width)
            blocks[pl.ds(4 * j, 4), deep_rows] = part
            return carry

        lax.fori_loop(0, 3, qkv_part, 0)
        part = dot(with_ones(o[...].reshape(width, 2 * slots).astype(BF16)), p[...])
        blocks[12:16, deep_rows] = part[:width].astype(BF16).reshape(4, deep, width)
        both = s[0] + s[1]
        rows = [
            both[A_GAIN_G : A_GAIN_G + 1], both[A_SHIFT_G : A_SHIFT_G + 1],
            lines_ref[0, :1], lines_ref[2, :1],
            part[width : width + 1],
            both[M_GAIN_G : M_GAIN_G + 1], both[M_SHIFT_G : M_SHIFT_G + 1],
            *[sums_ref[i, :1] for i in (4, 0, 1, 2, 3)],
        ]
        for i in range(CUTS):
            line = rows[i] if i < 12 else jnp.zeros((1, width), F32)
            blocks[i, deep:] = jnp.broadcast_to(line, (16, width)).astype(BF16)
            scatter.start(i, full)
        scatter.finish(full)

        @pl.when(lead)
        def _():
            g_copy.wait()

    ins = [(gain, "v")] + [(tokens, "a"), (weights[1], "a"), (weights[0], "a")]
    ins += [(dh, "a"), (grads, "a"), (sums, "v")]
    ins += [(kept[n], "a") for n in given]
    half = ((CUTS // 2, tall, width), BF16, "a")
    outs = [half, half, (grads.shape, grads.dtype, "a")]
    wshapes = weight_sizes(width, ff)
    scratch = [pltpu.VMEM(wshapes["out"], BF16), pltpu.VMEM(wshapes["qkv"], BF16)]
    scratch += [pltpu.VMEM(*shapes[n]) for n in names]
    scratch += [
        pltpu.VMEM((slots, width), BF16),
        pltpu.VMEM((2 * slots, width), BF16),
        pltpu.VMEM((3, HEADS, HEAD, 2 * slots), BF16),
        pltpu.VMEM((HEADS, HEAD, 2 * slots), F32),
        pltpu.VMEM((2 * slots, width), BF16),
        pltpu.VMEM((2, 8, width), F32),
        pltpu.VMEM((width + 16, 2 * slots), BF16),
        pltpu.VMEM((3, 8, width), F32),
    ]
    scratch += [
        pltpu.VMEM((CUTS, tall, width), BF16),
        pltpu.SemaphoreType.DMA((24,)),
        pltpu.SemaphoreType.DMA((CUTS,)),
    ]
    return run(body, ins, outs, scratch, {1 + 4: 2}, us=12, limit=MID)


def block(own, other, p):
    place = jnp.bitwise_xor(p, own_place())
    mine = own[place // 2]
    theirs = other[place // 2]
    odd = jnp.bitwise_and(place, 1)
    return jnp.where(odd == 1, theirs, mine).astype(F32)


def mlp_out(own, other, dims):
    slots, width, ff = dims
    deep = width // 4

    def body(own_ref, other_ref, down, up, token):
        token[...] = jnp.zeros((8, LANES), F32)
        for j in range(4):
            part = [block(own_ref, other_ref, 4 * j + i) for i in range(4)]
            down[0, j * width : (j + 1) * width, :] = jnp.concatenate(
                [v[:deep] for v in part], 0
            ).T
            up[0, :, j * width : (j + 1) * width] = jnp.concatenate([v[deep:] for v in part], 0)

    outs = [((1, ff, width), F32, "v"), ((1, width, ff), F32, "v"), ((8, LANES), F32, "v")]
    return run(body, [(own, "v"), (other, "v")], outs, [], us=4)


def attention_out(own, other, dims):
    slots, width, ff = dims
    deep = width // 4

    def body(own_ref, other_ref, qkv, out, *lines):
        for p in range(CUTS):
            j, i = p // 4, p % 4
            got = block(own_ref, other_ref, p)
            if j < 3:
                qkv[0, i * deep : (i + 1) * deep, j * width : (j + 1) * width] = got[:deep]
            else:
                out[0, i * deep : (i + 1) * deep, :] = got[:deep]
            if p < 8:
                lines[p][...] = got[deep : deep + 1]
            elif p < 12:
                lines[8][:, (p - 8) * width : (p - 7) * width] = got[deep : deep + 1]

    outs = [((1, width, 3 * width), F32, "v"), ((1, width, width), F32, "v")]
    outs += [((1, width), F32, "v")] * 8 + [((1, ff), F32, "v")]
    return run(body, [(own, "v"), (other, "v")], outs, [], us=3)


def swapped(x, bits):
    return lax.ppermute(x, "dp", [(i, i ^ bits) for i in range(CUTS)])


def added(*parts):
    total = parts[0].astype(F32)
    for x in parts[1:]:
        total = total + x.astype(F32)
    return total.astype(BF16)


def tied(token, *xs):
    return lax.optimization_barrier((token, *xs))[1:]


def square_send(u):
    return [swapped(u[:, j], 2 * j) for j in (1, 2, 3)]


def square_gather(u):
    return [swapped(u, 2 * j) for j in (1, 2, 3)]


def shards(
    tokens, cotangent, views, attn_gain, attn_shift, qkv_weight, query_bias, value_bias,
    out_weight, out_bias, mlp_gain, mlp_shift, up_weight, up_bias, down_weight, down_bias,
):
    dims = (tokens.shape[2], tokens.shape[3], up_bias.shape[1])
    weights = (qkv_weight, out_weight, up_weight, down_weight)
    lines = (
        attn_gain, attn_shift, query_bias, value_bias, out_bias, mlp_gain, mlp_shift, down_bias,
        up_bias,
    )

    counts = views[:, 0]

    def advance(t, carry):
        recv, bufs = carry
        step = jnp.reshape(t, (1,))
        send, bufs = cell(step, counts, lines, tokens, cotangent, recv, weights, bufs, dims)
        return lax.ppermute(send, "section", [(0, 1), (1, 0)]), bufs

    recv, bufs = lax.fori_loop(0, STEPS, advance, blank(dims))
    outs, grads = bufs[:2]
    kept = dict(zip(SAVED + TERMS, bufs[2:]))
    m_keep, m_send, sums, kept["dp"], kept["small"], dh = mlp_grads(
        mlp_gain, recv, weights, kept, dims
    )
    if lax.axis_size("dp") != CUTS:
        a_keep, a_send, grads = attention_grads(attn_gain, tokens, weights, kept, dh, grads, sums, dims)
        m, m_other, a, a_other = lax.psum((m_keep, m_send, a_keep, a_send), "dp")
        g_down, g_up, _ = mlp_out(m, m_other, dims)
    else:
        m = added(m_keep, swapped(m_send, 1)).reshape(2, 4, *m_keep.shape[1:])
        m1 = square_send(m)
        (dh,) = tied(m, dh)
        a_keep, a_send, grads = attention_grads(attn_gain, tokens, weights, kept, dh, grads, sums, dims)
        a_got = jnp.concatenate([swapped(v, 1) for v in jnp.split(a_send, 2)], 0)
        m1 = tied(a_keep, *m1)
        m = added(m[:, 0], *m1)
        m2 = swapped(m, 8)
        (a_got,) = tied(m, a_got)
        a = added(a_keep, a_got).reshape(2, 4, *a_keep.shape[1:])
        a1 = square_send(a)
        m2, *a1 = lax.optimization_barrier((m2, *a1))
        m = added(m, m2[::-1])
        m1 = square_gather(m)
        a = added(a[:, 0], *a1)
        a2 = swapped(a, 8)
        (a2,) = tied(m, a2)
        a = added(a, a2[::-1])
        a1 = square_gather(a)
        m1 = tied(a, *m1)
        m = jnp.stack([m, *m1], 1).reshape(8, *m.shape[1:])
        g_down, g_up, token = mlp_out(m, swapped(m, 1), dims)
        a1 = tied(token, *a1)
        a = jnp.stack([a, *a1], 1).reshape(8, *a.shape[1:])
        a_other = swapped(a, 1)
    g_qkv, g_out, *rows = attention_out(a, a_other, dims)
    g_ag, g_as, g_qb, g_vb, g_ob, g_mg, g_ms, g_db, g_ub = rows
    return (
        outs[None, :, None], grads[None, :, None], g_ag, g_as, g_qkv, g_qb, g_vb, g_out, g_ob,
        g_mg, g_ms, g_up, g_ub, g_down, g_db,
    )


def solution(mesh):
    scene = P(None, "dp", None, None)
    line = P("section", None)
    table = P("section", None, None)
    kept = P("section", None, "dp", None, None)
    kinds = (line, line, table, line, line, table, line, line, line, table, line, table, line)
    return jax.shard_map(
        shards,
        mesh=mesh,
        in_specs=(scene, scene, P(None, "dp")) + kinds,
        out_specs=(kept, kept) + kinds,
        check_vma=False,
    )
```
